1024 devices in a mesh: dp: 64 (over y, z), expert: 16 (over x, core).
Axes of the slice: x: 8, y: 8, z: 8, core: 2. Of those that a mesh axis runs over, the one named last changes fastest.
Arguments:
- image_tokens: bfloat16 [1024, 256, 640], P(('dp', 'expert'))
- text_tokens: bfloat16 [1024, 16, 640], P(('dp', 'expert'))
- text_counts: int32 [1024], P(('dp', 'expert')), may hold values from 3 to 16, as said below
- pair_labels: int32 [1024], P(('dp', 'expert')), may hold values from 0 to 1023, as said below
- image_expert: int32 [1024, 256], P(('dp', 'expert')), may hold values from 0 to 15
- image_rank: int32 [1024, 256], P(('dp', 'expert')), may hold values from 0 to 20, as said below
- image_keep: int32 [1024, 256], P(('dp', 'expert')), may hold values from 0 to 1, as said below
- text_expert: int32 [1024, 16], P(('dp', 'expert')), may hold values from 0 to 15
- text_rank: int32 [1024, 16], P(('dp', 'expert')), may hold values from 0 to 2, as said below
- text_keep: int32 [1024, 16], P(('dp', 'expert')), may hold values from 0 to 1, as said below
- image_gate: float32 [1024, 256], P(('dp', 'expert')), may hold values from 0.2 to 1
- text_gate: float32 [1024, 16], P(('dp', 'expert')), may hold values from 0.2 to 1
- w_in: bfloat16 [16, 640, 2560], P('expert'), may hold values from -0.25 to 0.25
- w_out: bfloat16 [16, 2560, 640], P('expert'), may hold values from -0.125 to 0.125
Outputs:
- image_out: bfloat16 [1024, 256, 640], P(('dp', 'expert'))
- text_out: bfloat16 [1024, 16, 640], P(('dp', 'expert'))
- image_grad: float32 [1024, 640], P(('dp', 'expert'))
- text_grad: float32 [1024, 640], P(('dp', 'expert'))
The draws below stay inside these ranges and needn't reach their ends.
Inputs may be any that keep to these rules, and one draw needn't show every extreme that they name: `text_counts`: every text has at least 3 valid tokens. `pair_labels`: each text index appears once. `image_rank`: the token's place, in batch-priority order, among the image tokens of its pair routed to the same expert, and 20 for every place past 20. In every aligned group of 16 blocks some expert holds 20 image tokens and 2 text tokens from each block. `image_keep`: 1 exactly where image_rank < 20. `text_rank`: the token's place, in order of position, among the valid text tokens of its pair routed to the same expert, 2 past 2 and for tokens past text_counts. `text_keep`: 1 exactly where text_rank < 2.
All inputs are finite; a program needn't handle non-finite values.
Results may differ from the reference program's by a relative error of at most 0.02.
Values may be sent and summed in bfloat16 or wider, within the bound.
No kernel may reach another device: no remote copies, remote signals or barrier semaphores. Data moves between devices by JAX's collectives and lax.ppermute only.
A program may use at most 32 MiB of HBM per device.

```python
import math
import jax
import jax.numpy as jnp
from jax import lax

D = 640
FF = 2560
IMG_TOK = 256
TXT_TOK = 16
PAIRS_DEV = 1
EXPERTS = 16
PAIRS = 1024
BATCH = 1024
CAP_IMG = 20
CAP_TXT = 2
SLOTS = 22
N_DP = 64
N_EXPERT = 16


def shared_pairs(key):
    perms = jax.random.permutation(jax.random.fold_in(key, 101), PAIRS).astype(jnp.int32)
    content = jax.random.normal(jax.random.fold_in(key, 102), (PAIRS, D), jnp.float32)
    strength = jax.random.uniform(jax.random.fold_in(key, 103), (PAIRS, 1), jnp.float32, 0.5, 1.5)
    content = content * strength
    return (perms, content)


def text_content_of(perms, content):
    return jnp.zeros_like(content).at[perms].set(content)


def place_ranks(choices, limit):
    onehot_table = (choices[:, :, None] == jnp.arange(EXPERTS, dtype=jnp.int32)[None, None, :]).astype(jnp.int32)
    before = jnp.cumsum(onehot_table, axis=1) - onehot_table
    return jnp.minimum(jnp.sum(before * onehot_table, axis=2), limit)


def route_tables(key):
    devices = PAIRS // PAIRS_DEV
    img_rows = PAIRS_DEV * IMG_TOK
    txt_rows = PAIRS_DEV * TXT_TOK
    row_hot = jax.random.randint(jax.random.fold_in(key, 201), (devices // EXPERTS,), 0, EXPERTS)
    hot_expert = jnp.repeat(row_hot, EXPERTS)
    device_keys = jax.random.split(jax.random.fold_in(key, 202), devices)
    priority = jax.vmap(lambda single: jax.random.permutation(single, img_rows))(device_keys).astype(jnp.int32)
    spread = jax.random.randint(jax.random.fold_in(key, 203), (devices, img_rows), 0, EXPERTS)
    position = jnp.arange(img_rows, dtype=jnp.int32)[None, :]
    by_place = jnp.where(position <= CAP_IMG, hot_expert[:, None], spread)
    rank_place = place_ranks(by_place, CAP_IMG)
    device_idx = jnp.arange(devices, dtype=jnp.int32)[:, None]
    img_expert = jnp.zeros((devices, img_rows), jnp.int32).at[device_idx, priority].set(by_place)
    img_rank = jnp.zeros((devices, img_rows), jnp.int32).at[device_idx, priority].set(rank_place)
    img_keep = (img_rank < CAP_IMG).astype(jnp.int32)
    text_counts = jax.random.randint(jax.random.fold_in(key, 204), (PAIRS,), 3, TXT_TOK + 1).at[0].set(TXT_TOK)
    valid_flags = (jnp.arange(TXT_TOK, dtype=jnp.int32)[None, :] < text_counts[:, None]).astype(jnp.int32).reshape(devices, txt_rows)
    valid_place = jnp.cumsum(valid_flags, axis=1) - valid_flags
    spread_text = jax.random.randint(jax.random.fold_in(key, 205), (devices, txt_rows), 0, EXPERTS)
    txt_expert = jnp.where((valid_flags == 1) & (valid_place <= CAP_TXT), hot_expert[:, None], spread_text)
    onehot_text = (txt_expert[:, :, None] == jnp.arange(EXPERTS, dtype=jnp.int32)[None, None, :]).astype(jnp.int32) * valid_flags[:, :, None]
    before = jnp.cumsum(onehot_text, axis=1) - onehot_text
    txt_rank = jnp.where(valid_flags == 1, jnp.minimum(jnp.sum(before * onehot_text, axis=2), CAP_TXT), CAP_TXT)
    txt_keep = (txt_rank < CAP_TXT).astype(jnp.int32)
    return (img_expert.reshape(PAIRS, IMG_TOK), img_rank.reshape(PAIRS, IMG_TOK), img_keep.reshape(PAIRS, IMG_TOK), txt_expert.reshape(PAIRS, TXT_TOK), txt_rank.reshape(PAIRS, TXT_TOK), txt_keep.reshape(PAIRS, TXT_TOK), text_counts)


def draw_pair_labels(key, part):
    perms, content = shared_pairs(key)
    return perms


def draw_image_tokens(key, part):
    perms, content = shared_pairs(key)
    key = jax.random.fold_in(key, 1)
    noise_part = 0.6 * jax.random.normal(key, (PAIRS, IMG_TOK, D), jnp.float32)
    return (content[:, None, :] + noise_part).astype(jnp.bfloat16)


def draw_text_tokens(key, part):
    perms, content = shared_pairs(key)
    key = jax.random.fold_in(key, 2)
    noise_part = 0.6 * jax.random.normal(key, (PAIRS, TXT_TOK, D), jnp.float32)
    text_content = text_content_of(perms, content)
    return (text_content[:, None, :] + noise_part).astype(jnp.bfloat16)


def draw_text_counts(key, part):
    tables = route_tables(key)
    return tables[6]


def draw_image_expert(key, part):
    tables = route_tables(key)
    return tables[0]


def draw_image_rank(key, part):
    tables = route_tables(key)
    return tables[1]


def draw_image_keep(key, part):
    tables = route_tables(key)
    return tables[2]


def draw_text_expert(key, part):
    tables = route_tables(key)
    return tables[3]


def draw_text_rank(key, part):
    tables = route_tables(key)
    return tables[4]


def draw_text_keep(key, part):
    tables = route_tables(key)
    return tables[5]


def block_scale(key, extent, cuts, smallest, largest):
    def one(axis_at, parts):
        draws = jax.random.uniform(jax.random.fold_in(jax.random.fold_in(key, 6), axis_at), (parts,), jnp.float32, smallest / len(cuts), largest / len(cuts))
        return jnp.repeat(jnp.exp(draws), extent[axis_at] // parts).reshape((-1,) + (1,) * (len(extent) - axis_at - 1))

    gain = one(*cuts[0])
    for cut in cuts[1:]:
        gain = gain * one(*cut)
    return gain


def scatter_about(rng, extent, deviation, bound, cuts=(), held_as=jnp.bfloat16):
    loudness = block_scale(rng, extent, cuts, -0.22, 0.18) if cuts else 1.0
    array = jax.random.normal(rng, extent, jnp.float32) * deviation * loudness
    return jnp.minimum(jnp.maximum(array, -bound), bound).astype(held_as)


def setup_inputs(seed: int = 0) -> dict:
    arg_keys = jax.random.split(jax.random.key(seed), 15)
    return {
        "image_tokens": draw_image_tokens(jax.random.fold_in(arg_keys[14], 71), 0),
        "text_tokens": draw_text_tokens(jax.random.fold_in(arg_keys[14], 71), 0),
        "text_counts": draw_text_counts(jax.random.fold_in(arg_keys[14], 71), 0),
        "pair_labels": draw_pair_labels(jax.random.fold_in(arg_keys[14], 71), 0),
        "image_expert": draw_image_expert(jax.random.fold_in(arg_keys[14], 71), 0),
        "image_rank": draw_image_rank(jax.random.fold_in(arg_keys[14], 71), 0),
        "image_keep": draw_image_keep(jax.random.fold_in(arg_keys[14], 71), 0),
        "text_expert": draw_text_expert(jax.random.fold_in(arg_keys[14], 71), 0),
        "text_rank": draw_text_rank(jax.random.fold_in(arg_keys[14], 71), 0),
        "text_keep": draw_text_keep(jax.random.fold_in(arg_keys[14], 71), 0),
        "image_gate": jnp.clip(jnp.exp(math.log(1.0) - 1.609438 * jax.random.uniform(arg_keys[10], (PAIRS, IMG_TOK), jnp.float32) ** block_scale(arg_keys[10], (PAIRS, IMG_TOK), ((0, 1024),), -0.2, 0.2)), 0.2, 1.0),
        "text_gate": jnp.clip(jnp.exp(math.log(1.0) - 1.609438 * jax.random.uniform(arg_keys[11], (PAIRS, TXT_TOK), jnp.float32) ** block_scale(arg_keys[11], (PAIRS, TXT_TOK), ((0, 1024),), -0.2, 0.2)), 0.2, 1.0),
        "w_in": scatter_about(arg_keys[12], (EXPERTS, D, FF), D ** -0.5, 0.25, ((0, 16),)),
        "w_out": scatter_about(arg_keys[13], (EXPERTS, FF, D), FF ** -0.5, 0.125, ((0, 16),)),
    }


logit_scale = 10.0

def contrast_batch(image_emb, text_emb, labels):
    logits = logit_scale * jnp.dot(image_emb, text_emb.T, preferred_element_type=jnp.float32)
    exp_scores = jnp.exp(logits)
    row_totals = lax.optimization_barrier(jnp.sum(exp_scores, axis=1))
    column_totals = lax.optimization_barrier(jnp.sum(exp_scores, axis=0))
    matches = (jnp.arange(BATCH, dtype=jnp.int32)[None, :] == labels[:, None]).astype(jnp.float32)
    scores = (exp_scores / row_totals[:, None] + exp_scores / column_totals[None, :] - 2.0 * matches).astype(jnp.bfloat16)
    image_grad = jnp.dot(scores, text_emb, preferred_element_type=jnp.float32)
    text_grad = jnp.dot(scores.T, image_emb, preferred_element_type=jnp.float32)
    return (image_grad, text_grad)

def reference(image_tokens, text_tokens, text_counts, pair_labels, image_expert, image_rank, image_keep, text_expert, text_rank, text_keep, image_gate, text_gate, w_in, w_out):
    devices = N_DP * N_EXPERT
    img_rows = PAIRS_DEV * IMG_TOK
    txt_rows = PAIRS_DEV * TXT_TOK
    all_rows = img_rows + txt_rows
    tokens = jnp.concatenate([image_tokens.reshape(devices, img_rows, D), text_tokens.reshape(devices, txt_rows, D)], 1)
    target = jnp.concatenate([image_expert.reshape(devices, img_rows) * SLOTS + image_rank.reshape(devices, img_rows), text_expert.reshape(devices, txt_rows) * SLOTS + CAP_IMG + text_rank.reshape(devices, txt_rows)], 1).astype(jnp.int32)
    keep_flags = jnp.concatenate([image_keep.reshape(devices, img_rows), text_keep.reshape(devices, txt_rows)], 1)
    gate_vals = jnp.concatenate([image_gate.reshape(devices, img_rows), text_gate.reshape(devices, txt_rows)], 1)
    tokens = tokens.reshape(N_DP, N_EXPERT, all_rows, D)
    target = target.reshape(N_DP, N_EXPERT, all_rows)
    keep_flags = keep_flags.reshape(N_DP, N_EXPERT, all_rows)
    gate_vals = gate_vals.reshape(N_DP, N_EXPERT, all_rows)
    weight_in = w_in.astype(jnp.float32)
    weight_out = w_out.astype(jnp.float32)

    def one_group(pieces):
        group_tokens, group_target, group_keep, group_gate = pieces
        columns = jnp.arange(EXPERTS * SLOTS, dtype=jnp.int32)
        dispatch = ((group_target[:, :, None] == columns[None, None, :]) & (group_keep[:, :, None] == 1)).astype(jnp.float32)
        packed = jnp.einsum('srk,srd->skd', dispatch, group_tokens.astype(jnp.float32)).astype(jnp.bfloat16)
        packed = packed.reshape(N_EXPERT, EXPERTS, SLOTS, D).transpose(1, 0, 2, 3).reshape(EXPERTS, N_EXPERT * SLOTS, D)
        hidden = jnp.einsum('end,edf->enf', packed.astype(jnp.float32), weight_in)
        hidden = jax.nn.gelu(hidden, approximate=False).astype(jnp.bfloat16)
        result = jnp.einsum('enf,efd->end', hidden.astype(jnp.float32), weight_out).astype(jnp.bfloat16)
        returned = result.reshape(EXPERTS, N_EXPERT, SLOTS, D).transpose(1, 0, 2, 3).reshape(N_EXPERT, EXPERTS * SLOTS, D)
        picked = jnp.einsum('srk,skd->srd', dispatch, returned.astype(jnp.float32))
        return group_tokens.astype(jnp.float32) + group_gate[:, :, None] * picked
    combined = lax.map(one_group, (tokens, target, keep_flags, gate_vals)).reshape(devices, all_rows, D)
    image_part = combined[:, :img_rows].reshape(PAIRS, IMG_TOK, D)
    text_part = combined[:, img_rows:].reshape(PAIRS, TXT_TOK, D)
    image_out = image_part.astype(jnp.bfloat16)
    text_out = text_part.astype(jnp.bfloat16)
    image_pool = lax.optimization_barrier(jnp.mean(image_part, axis=1))
    valid_flags = (jnp.arange(TXT_TOK, dtype=jnp.int32)[None, :] < text_counts[:, None]).astype(jnp.float32)
    text_pool = lax.optimization_barrier(jnp.sum(text_part * valid_flags[:, :, None], axis=1)) / text_counts.astype(jnp.float32)[:, None]
    image_emb = (image_pool / jnp.sqrt(lax.optimization_barrier(jnp.sum(image_pool * image_pool, axis=1, keepdims=True)) + 1e-06)).astype(jnp.bfloat16)
    text_emb = (text_pool / jnp.sqrt(lax.optimization_barrier(jnp.sum(text_pool * text_pool, axis=1, keepdims=True)) + 1e-06)).astype(jnp.bfloat16)
    image_grad, text_grad = contrast_batch(image_emb, text_emb, pair_labels)
    return (image_out, text_out, image_grad, text_grad)
```

```python
import jax
import jax.numpy as jnp
import numpy as np
from jax import lax
from jax.experimental import pallas as pl
from jax.experimental.pallas import tpu as pltpu
from jax.sharding import PartitionSpec as P

logit_scale = 10.0
f32, bf16, i32 = jnp.float32, jnp.bfloat16, jnp.int32
NT = (((1,), (1,)), ((), ()))
TN = (((0,), (0,)), ((), ()))
NN = (((1,), (0,)), ((), ()))


def dot(left, right, dims=NN):
    return lax.dot_general(left, right, dims, preferred_element_type=f32)


def iota(shape, dim):
    return lax.broadcasted_iota(i32, shape, dim)


def one_hot(mask):
    return jnp.where(mask, 1.0, 0.0).astype(bf16)


def three_parts(value):
    high = value.astype(bf16)
    rest = value - high.astype(f32)
    middle = rest.astype(bf16)
    low = (rest - middle.astype(f32)).astype(bf16)
    return high, middle, low


class Sizes:
    def __init__(self, owners, lines, img_tok, txt_tok, feat):
        self.owners, self.lines = owners, lines
        self.cores = 2
        self.nx = owners // self.cores
        self.ny = 1 << ((lines.bit_length() - 1 + 1) // 2)
        self.nz = lines // self.ny
        self.img_tok, self.txt_tok, self.feat = img_tok, txt_tok, feat
        self.cap = 5 * img_tok // (4 * owners)
        self.slots = self.cap + 2
        self.stride = -(-(self.slots + 2) // 8) * 8
        self.rows = owners * self.stride
        self.half = self.nx * lines
        self.pairs = owners * lines


def slot_masks(sz, img_expert, img_rank, img_keep, txt_expert, txt_rank, txt_keep):
    img_target = img_expert * sz.stride + img_rank
    txt_target = txt_expert * sz.stride + sz.cap + txt_rank
    img_target = jnp.where(img_keep == 1, img_target, -1)
    txt_target = jnp.where(txt_keep == 1, txt_target, -1)
    return (
        one_hot(iota((sz.rows, sz.img_tok), 0) == img_target),
        one_hot(iota((sz.rows, sz.txt_tok), 0) == txt_target),
    )


def dispatch_kernel(sz, count_ref, label_ref, ie, ir, ik, te, tr, tk, ig, tg, img, txt, packed, means):
    img_mask, txt_mask = slot_masks(sz, ie[...], ir[...], ik[...], te[...], tr[...], tk[...])
    count = count_ref[0]
    count_f = jnp.full((1, 1), count, i32).astype(f32)
    label = label_ref[0]
    img_weight = jnp.where(ik[...] == 1, ig[...], 0.0) * (1.0 / sz.img_tok)
    valid = iota((1, sz.txt_tok), 1) < count
    txt_weight = jnp.where((tk[...] == 1) & valid, tg[...], 0.0) / count_f
    img_place = one_hot(iota((128, sz.img_tok), 0) == ir[...])
    txt_place = one_hot(iota((128, sz.txt_tok), 0) == tr[...] + sz.cap)
    img_at = iota((sz.owners, sz.img_tok), 0) == ie[...]
    txt_at = iota((sz.owners, sz.txt_tok), 0) == te[...]
    tables = []
    for img_part, txt_part in zip(three_parts(img_weight), three_parts(txt_weight)):
        img_side = jnp.where(img_at, img_part.astype(f32), 0.0).astype(bf16)
        txt_side = jnp.where(txt_at, txt_part.astype(f32), 0.0).astype(bf16)
        tables.append(dot(img_side, img_place, NT) + dot(txt_side, txt_place, NT))
    pad = sz.feat - 3 * 128
    if pad:
        tables.append(jnp.zeros((sz.owners, pad), f32))
    weights = jnp.concatenate(tables, 1).astype(bf16)
    lane = iota((sz.owners, sz.feat), 1)
    label_row = jnp.where(
        lane < 128,
        (label >> 5).astype(f32),
        jnp.where(lane < 256, (label & 31).astype(f32), 0.0),
    ).astype(bf16)
    row = iota((sz.rows, sz.owners), 0)
    block = iota((sz.rows, sz.owners), 1) * sz.stride
    out = dot(img_mask, img[...]) + dot(txt_mask, txt[...])
    out = out + dot(one_hot(row == block + sz.slots), weights)
    out = out + dot(one_hot(row == block + sz.slots + 1), label_row)
    packed[...] = out.astype(bf16)
    img_mean = dot(jnp.ones((8, sz.img_tok), bf16), img[...]) * (1.0 / sz.img_tok)
    counted = one_hot(iota((8, sz.txt_tok), 1) < count)
    txt_mean = dot(counted, txt[...]) / count_f
    means[...] = jnp.where(iota((8, sz.feat), 0) == 0, img_mean, txt_mean)


def gelu(x):
    return 0.5 * x * (1.0 + lax.erf(x * np.float32(np.sqrt(0.5))))


def expert_kernel(sz, chunk, x_ref, w_in, w_out, means, rows_ref, pool_ref, label_ref, total):
    step = pl.program_id(0)

    @pl.when(step == 0)
    def _():
        total[...] = jnp.zeros_like(total)

    x = x_ref[...]
    width = w_in.shape[1]
    part = None
    for at in range(0, width, chunk):
        hidden = gelu(dot(x, w_in[:, at : at + chunk])).astype(bf16)
        term = dot(hidden, w_out[at : at + chunk, :])
        part = term if part is None else part + term
    total[...] += part

    @pl.when(step == pl.num_programs(0) - 1)
    def _():
        out = total[...].astype(bf16)
        rows_ref[...] = out
        count = 2 * sz.owners
        r = iota((count, sz.rows), 0)
        c = iota((count, sz.rows), 1)
        magic = -(-65536 // sz.stride)
        assert all((v * magic) >> 16 == v // sz.stride for v in range(sz.rows))
        block = (c * magic) >> 16
        place = c - block * sz.stride
        is_txt = (r & sz.nx) > 0
        source = (r & (sz.nx - 1)) * sz.cores + jnp.where(r >= 2 * sz.nx, 1, 0)
        held = dot(one_hot(c == source * sz.stride + sz.slots), x)
        lane = iota((128, sz.rows), 1)
        lane_place = lane - ((lane * magic) >> 16) * sz.stride
        spread = one_hot(iota((128, sz.rows), 0) == lane_place)
        own = (block == source) & (
            jnp.where(is_txt, 1, 0) == jnp.where(place >= sz.cap, 1, 0)
        ) & (place < sz.slots)
        pool = jnp.zeros((count, sz.feat), f32)
        for part_at in range(3):
            piece = held[:, part_at * 128 : (part_at + 1) * 128].astype(bf16)
            weight = jnp.where(own, dot(piece, spread), 0.0).astype(bf16)
            pool = pool + dot(weight, out)
        me = lax.axis_index("expert")
        line = lax.axis_index("dp")
        my_x, my_core = me >> 1, me & 1
        row = iota((count, sz.feat), 0)
        my_row = my_core * (2 * sz.nx) + my_x
        pool = pool + jnp.where(row == my_row, means[0:1, :], 0.0)
        pool = pool + jnp.where(row == my_row + sz.nx, means[1:2, :], 0.0)
        pool_ref[...] = pool
        r8 = iota((sz.nx, sz.rows), 0)
        c8 = iota((sz.nx, sz.rows), 1)
        labels = dot(one_hot(c8 == (r8 * sz.cores + my_core) * sz.stride + sz.slots + 1), x)
        lane = iota((sz.nx, sz.feat), 1)
        label_ref[...] = jnp.where((lane == line) | (lane == line + 128), labels, 0.0).astype(bf16)


def normalize_kernel(sz, mine, theirs, label, out):
    pooled = mine[...] + theirs[...]
    norm = jnp.sqrt(jnp.sum(pooled * pooled, axis=1, keepdims=True) + 1e-06)
    out[...] = jnp.concatenate([(pooled / norm).astype(bf16), label[...]], 0)


def combine_kernel(sz, ie, ir, ik, te, tr, tk, ig, tg, img, txt, returned, img_out, txt_out):
    img_mask, txt_mask = slot_masks(sz, ie[...], ir[...], ik[...], te[...], tr[...], tk[...])
    back = returned[...]
    for mask, gate, tokens, out in ((img_mask, ig, img, img_out), (txt_mask, tg, txt, txt_out)):
        count = tokens.shape[0]
        picked = dot(mask, back, TN)
        column = jnp.transpose(jnp.broadcast_to(gate[...], (128, count)))[:, 0:1]
        out[...] = (tokens[...].astype(f32) + column * picked).astype(bf16)


def reverse(value, width):
    bits = [((value >> b) & 1) << (width - 1 - b) for b in range(width)]
    out = bits[0]
    for b in bits[1:]:
        out = out | b
    return out


def merge_kernel(count, held, got, out):
    out[...] = jnp.concatenate(
        [
            held[:count, :],
            got[:count, :],
            held[count : 2 * count, :],
            got[count : 2 * count, :],
            held[2 * count :, :] + got[2 * count :, :],
        ],
        0,
    )


def head_kernel(sz, label_ref, mine_held, mine_got, theirs_held, theirs_got, img_grad, txt_grad, column_scores):
    half = sz.half
    tile = half // 2
    me = lax.axis_index("expert")
    line = lax.axis_index("dp")
    my_x, my_core = me >> 1, me & 1
    y_bits, z_bits = sz.ny.bit_length() - 1, sz.nz.bit_length() - 1
    pair = line * sz.owners + me

    def position(other_line, other_x, other_core):
        apart_y = reverse((other_line >> z_bits) ^ (line >> z_bits), y_bits)
        apart_z = reverse((other_line & (sz.nz - 1)) ^ (line & (sz.nz - 1)), z_bits)
        block = jnp.where(
            other_core == 0, apart_y | (apart_z << y_bits), apart_z | (apart_y << z_bits)
        )
        return jnp.where(other_core == my_core, 0, half) + block * sz.nx + other_x

    parts = (mine_held, mine_got, theirs_held, theirs_got)
    width = column_scores.shape[1]
    column_totals = [jnp.zeros((1, tile), f32) for _ in parts]
    row_totals = []
    strip = []
    for a, left in enumerate(parts):
        images = left[:tile, :]
        sums = jnp.zeros((tile, 1), f32)
        for b, right in enumerate(parts):
            scores = jnp.exp(logit_scale * dot(images, right[tile : 2 * tile, :], NT))
            sums = sums + jnp.sum(scores, axis=1, keepdims=True)
            column_totals[b] = column_totals[b] + jnp.sum(scores, axis=0, keepdims=True)
            if b == 0:
                column_scores[a * tile : (a + 1) * tile, :] = scores[:, :width]
            if a == 0:
                strip.append(scores[: sz.nx, :])
        row_totals.append(sums)

    label = label_ref[0]
    owner = label & (sz.owners - 1)
    target = position(label >> (sz.owners.bit_length() - 1), owner >> 1, owner & 1)
    grad = jnp.zeros((sz.nx, sz.feat), f32)
    for b, right in enumerate(parts):
        match = jnp.where(iota((sz.nx, tile), 1) + b * tile == target, 2.0, 0.0)
        scores = strip[b] / row_totals[0][: sz.nx] + strip[b] / column_totals[b] - match
        grad = grad + dot(scores.astype(bf16), right[tile : 2 * tile, :])
    chosen = iota((sz.nx, sz.feat), 0) == my_x
    img_grad[...] = jnp.sum(jnp.where(chosen, grad, 0.0), axis=0, keepdims=True)

    lane = iota((sz.nx, 128), 1)
    sub = iota((sz.nx, 128), 0)
    found_line = jnp.zeros((1, 1), i32)
    found_x = jnp.zeros((1, 1), i32)
    found_theirs = jnp.zeros((1, 1), i32)
    high, low = (pair >> 5).astype(f32), (pair & 31).astype(f32)
    for b in range(2):
        held, got = parts[2 * b], parts[2 * b + 1]
        names = held[2 * tile :, 0:256].astype(f32) + got[2 * tile :, 0:256].astype(f32)
        hit = (names[:, :128] == high) & (names[:, 128:] == low) & (lane < sz.lines)

        def total(value):
            value = jnp.where(hit, value, 0.0)
            return jnp.sum(jnp.sum(value, axis=0, keepdims=True), axis=1, keepdims=True).astype(i32)

        found_line = found_line + total(lane.astype(f32))
        found_x = found_x + total(sub.astype(f32))
        if b == 1:
            found_theirs = total(jnp.ones((sz.nx, 128), f32))
    found_core = jnp.where(found_theirs > 0, 1 - my_core, my_core)
    named = position(found_line, found_x, found_core)
    grad = jnp.zeros((width, sz.feat), f32)
    for a, left in enumerate(parts):
        rows = column_scores[a * tile : (a + 1) * tile, :]
        match = jnp.where(iota((tile, width), 0) + a * tile == named, 2.0, 0.0)
        scores = rows / row_totals[a] + rows / column_totals[0][:, :width] - match
        grad = grad + dot(scores.astype(bf16), left[:tile, :], TN)
    txt_grad[...] = jnp.sum(jnp.where(chosen, grad[: sz.nx], 0.0), axis=0, keepdims=True)


def call(kernel, out_shape, in_specs=None, cost=None, limit=24, **kw):
    if cost is not None:
        kw["cost_estimate"] = pl.CostEstimate(flops=cost[0], bytes_accessed=cost[1], transcendentals=cost[2])
    if in_specs is not None:
        kw["in_specs"] = in_specs
    return pl.pallas_call(
        kernel,
        out_shape=out_shape,
        compiler_params=pltpu.CompilerParams(vmem_limit_bytes=limit << 20),
        **kw,
    )


def bind(kernel, *head):
    def bound(*refs):
        return kernel(*head, *refs)

    return bound


def swap(value, sz, partner):
    pairs = []
    for y in range(sz.ny):
        for z in range(sz.nz):
            for x in range(sz.nx):
                for core in range(sz.cores):
                    py, pz, px, pcore = partner(y, z, x, core)
                    rank = ((y * sz.nz + z) * sz.nx + x) * sz.cores + core
                    pairs.append((rank, ((py * sz.nz + pz) * sz.nx + px) * sz.cores + pcore))
    return lax.ppermute(value, ("dp", "expert"), pairs)


def masks(count):
    out = []
    while count > 1:
        count //= 2
        out.append(count)
    return out


def per_device(
    image_tokens,
    text_tokens,
    text_counts,
    pair_labels,
    image_expert,
    image_rank,
    image_keep,
    text_expert,
    text_rank,
    text_keep,
    image_gate,
    text_gate,
    w_in,
    w_out,
):
    _, img_tok, feat = image_tokens.shape
    txt_tok = text_tokens.shape[1]
    sz = Sizes(lax.axis_size("expert"), lax.axis_size("dp"), img_tok, txt_tok, feat)
    ff = w_in.shape[2]
    img, txt = image_tokens[0], text_tokens[0]
    routes = (image_expert, image_rank, image_keep, text_expert, text_rank, text_keep)
    gates = (image_gate, text_gate)
    vmem = pl.BlockSpec(memory_space=pltpu.VMEM)
    smem = pl.BlockSpec(memory_space=pltpu.SMEM)
    packed, means = call(
        bind(dispatch_kernel, sz),
        (
            jax.ShapeDtypeStruct((sz.rows, feat), bf16),
            jax.ShapeDtypeStruct((8, feat), f32),
        ),
        in_specs=[smem, smem] + [vmem] * 10,
        name="dispatch",
    )(text_counts, pair_labels, *routes, *gates, img, txt)

    def exchange(rows):
        rows = rows.reshape(sz.owners, sz.stride, feat)
        rows = lax.all_to_all(rows, "expert", split_axis=0, concat_axis=0, tiled=True)
        return rows.reshape(sz.rows, feat)

    received = exchange(packed)
    block = min(512, ff)
    whole = lambda shape: pl.BlockSpec(shape, lambda i: (0, 0))
    rows, pools, labels = call(
        bind(expert_kernel, sz, min(256, block)),
        (
            jax.ShapeDtypeStruct((sz.rows, feat), bf16),
            jax.ShapeDtypeStruct((2 * sz.owners, feat), f32),
            jax.ShapeDtypeStruct((sz.nx, feat), bf16),
        ),
        grid=(ff // block,),
        in_specs=[
            whole((sz.rows, feat)),
            pl.BlockSpec((feat, block), lambda i: (0, i)),
            pl.BlockSpec((block, feat), lambda i: (i, 0)),
            whole((8, feat)),
        ],
        out_specs=[
            whole((sz.rows, feat)),
            whole((2 * sz.owners, feat)),
            whole((sz.nx, feat)),
        ],
        scratch_shapes=[pltpu.VMEM((sz.rows, feat), f32)],
        name="expert",
    )(received, w_in[0], w_out[0], means)

    core = lax.axis_index("expert") & 1
    per_core = 2 * sz.nx
    mine = lax.dynamic_slice_in_dim(pools, core * per_core, per_core, 0)
    others = lax.dynamic_slice_in_dim(pools, (1 - core) * per_core, per_core, 0)
    theirs = swap(others, sz, lambda y, z, x, c: (y, z, x, 1 - c))
    for mask in masks(sz.nx):
        mine = mine + theirs
        theirs = swap(mine, sz, lambda y, z, x, c: (y, z, x ^ mask, c))
    held = call(
        bind(normalize_kernel, sz),
        jax.ShapeDtypeStruct((3 * sz.nx, feat), bf16),
        name="normalize",
    )(mine, theirs, labels)

    rows, held = lax.optimization_barrier((rows, held))
    returned = exchange(rows)
    img_out, txt_out = call(
        bind(combine_kernel, sz),
        (
            jax.ShapeDtypeStruct((img_tok, feat), bf16),
            jax.ShapeDtypeStruct((txt_tok, feat), bf16),
        ),
        cost=(2 * sz.rows * (img_tok + txt_tok) * feat, 4 * sz.rows * feat, 0),
        name="combine",
    )(*routes, *gates, img, txt, returned)

    def across(value):
        return swap(value, sz, lambda y, z, x, c: (y, z, x, 1 - c))

    count = sz.nx
    for second in (False, True):
        for y_mask, z_mask in zip(masks(sz.ny), masks(sz.nz)):

            def partner(y, z, x, c):
                if (c == 0) != second:
                    return (y ^ y_mask, z, x, c)
                return (y, z ^ z_mask, x, c)

            got = swap(held, sz, partner)
            if 2 * count < sz.half:
                held = call(
                    bind(merge_kernel, count),
                    jax.ShapeDtypeStruct((4 * count + sz.nx, feat), bf16),
                    name="merge",
                )(held, got)
            count *= 2
    img_grad, txt_grad = call(
        bind(head_kernel, sz),
        (
            jax.ShapeDtypeStruct((1, feat), f32),
            jax.ShapeDtypeStruct((1, feat), f32),
        ),
        in_specs=[smem] + [vmem] * 4,
        scratch_shapes=[pltpu.VMEM((2 * sz.half, min(128, sz.half // 2)), f32)],
        name="head",
    )(pair_labels, held, got, across(held), across(got))
    return (img_out[None], txt_out[None], img_grad, txt_grad)


def solution(mesh):
    both = ("dp", "expert")
    return jax.shard_map(
        per_device,
        mesh=mesh,
        in_specs=(
            P(both, None, None),
            P(both, None, None),
            P(both),
            P(both),
            P(both, None),
            P(both, None),
            P(both, None),
            P(both, None),
            P(both, None),
            P(both, None),
            P(both, None),
            P(both, None),
            P("expert", None, None),
            P("expert", None, None),
        ),
        out_specs=(
            P(both, None, None),
            P(both, None, None),
            P(both, None),
            P(both, None),
        ),
        check_vma=False,
    )
```

```python
import jax
import jax.numpy as jnp
import numpy as np
from jax import lax
from jax.experimental import pallas as pl
from jax.experimental.pallas import tpu as pltpu
from jax.sharding import PartitionSpec as P

logit_scale = 10.0
f32, bf16, i32 = jnp.float32, jnp.bfloat16, jnp.int32
NT = (((1,), (1,)), ((), ()))
TN = (((0,), (0,)), ((), ()))
NN = (((1,), (0,)), ((), ()))


def dot(left, right, dims=NN):
    return lax.dot_general(left, right, dims, preferred_element_type=f32)


def divided(value, by, limit):
    magic = -(-65536 // by)
    assert all((v * magic) >> 16 == v // by for v in range(limit))
    return (value * magic) >> 16


def iota(shape, dim):
    return lax.broadcasted_iota(i32, shape, dim)


def one_hot(mask):
    return jnp.where(mask, 1.0, 0.0).astype(bf16)


def three_parts(value):
    high = value.astype(bf16)
    rest = value - high.astype(f32)
    middle = rest.astype(bf16)
    low = (rest - middle.astype(f32)).astype(bf16)
    return high, middle, low


class Sizes:
    def __init__(self, owners, lines, img_tok, txt_tok, feat):
        self.owners, self.lines = owners, lines
        self.cores = 2
        self.nx = owners // self.cores
        self.ny = 1 << ((lines.bit_length() - 1 + 1) // 2)
        self.nz = lines // self.ny
        self.img_tok, self.txt_tok, self.feat = img_tok, txt_tok, feat
        self.cap = 5 * img_tok // (4 * owners)
        self.slots = self.cap + 2
        self.stride = -(-(self.slots + 2) // 8) * 8
        self.rows = owners * self.stride
        self.back = self.stride + 2 * self.nx
        self.half = self.nx * lines
        self.pairs = owners * lines


def slot_masks(sz, stride, img_expert, img_rank, img_keep, txt_expert, txt_rank, txt_keep):
    img_target = img_expert * stride + img_rank
    txt_target = txt_expert * stride + sz.cap + txt_rank
    img_target = jnp.where(img_keep == 1, img_target, -1)
    txt_target = jnp.where(txt_keep == 1, txt_target, -1)
    return (
        one_hot(iota((sz.owners * stride, sz.img_tok), 0) == img_target),
        one_hot(iota((sz.owners * stride, sz.txt_tok), 0) == txt_target),
    )


def dispatch_kernel(sz, count_ref, label_ref, ie, ir, ik, te, tr, tk, ig, tg, img, txt, packed, means):
    img_mask, txt_mask = slot_masks(sz, sz.stride, ie[...], ir[...], ik[...], te[...], tr[...], tk[...])
    count = count_ref[0]
    count_f = jnp.full((1, 1), count, i32).astype(f32)
    label = label_ref[0]
    img_weight = jnp.where(ik[...] == 1, ig[...], 0.0) * (1.0 / sz.img_tok)
    valid = iota((1, sz.txt_tok), 1) < count
    txt_weight = jnp.where((tk[...] == 1) & valid, tg[...], 0.0) / count_f
    img_place = one_hot(iota((128, sz.img_tok), 0) == ir[...])
    txt_place = one_hot(iota((128, sz.txt_tok), 0) == tr[...] + sz.cap)
    img_at = iota((sz.owners, sz.img_tok), 0) == ie[...]
    txt_at = iota((sz.owners, sz.txt_tok), 0) == te[...]
    tables = []
    for img_part, txt_part in zip(three_parts(img_weight), three_parts(txt_weight)):
        img_side = jnp.where(img_at, img_part.astype(f32), 0.0).astype(bf16)
        txt_side = jnp.where(txt_at, txt_part.astype(f32), 0.0).astype(bf16)
        tables.append(dot(img_side, img_place, NT) + dot(txt_side, txt_place, NT))
    pad = sz.feat - 3 * 128
    if pad:
        tables.append(jnp.zeros((sz.owners, pad), f32))
    weights = jnp.concatenate(tables, 1).astype(bf16)
    lane = iota((sz.owners, sz.feat), 1)
    label_row = jnp.where(
        lane < 128,
        (label >> 5).astype(f32),
        jnp.where(lane < 256, (label & 31).astype(f32), 0.0),
    ).astype(bf16)
    row = iota((sz.rows, sz.owners), 0)
    block = iota((sz.rows, sz.owners), 1) * sz.stride
    out = dot(img_mask, img[...]) + dot(txt_mask, txt[...])
    out = out + dot(one_hot(row == block + sz.slots), weights)
    out = out + dot(one_hot(row == block + sz.slots + 1), label_row)
    packed[...] = out.astype(bf16)
    img_mean = dot(jnp.ones((8, sz.img_tok), bf16), img[...]) * (1.0 / sz.img_tok)
    counted = one_hot(iota((8, sz.txt_tok), 1) < count)
    txt_mean = dot(counted, txt[...]) / count_f
    means[...] = jnp.where(iota((8, sz.feat), 0) == 0, img_mean, txt_mean)


def gelu(x):
    return 0.5 * x * (1.0 + lax.erf(x * np.float32(np.sqrt(0.5))))


def expert_kernel(sz, chunk, x_ref, w_in, w_out, means, back_ref, label_ref, total):
    step = pl.program_id(0)

    @pl.when(step == 0)
    def _():
        total[...] = jnp.zeros_like(total)

    x = x_ref[...]
    width = w_in.shape[1]
    part = None
    for at in range(0, width, chunk):
        hidden = gelu(dot(x, w_in[:, at : at + chunk])).astype(bf16)
        term = dot(hidden, w_out[at : at + chunk, :])
        part = term if part is None else part + term
    total[...] += part

    @pl.when(step == pl.num_programs(0) - 1)
    def _():
        out = total[...].astype(bf16)
        count = 2 * sz.owners
        r = iota((count, sz.rows), 0)
        c = iota((count, sz.rows), 1)
        block = divided(c, sz.stride, sz.rows)
        place = c - block * sz.stride
        is_txt = (r & sz.nx) > 0
        source = (r & (sz.nx - 1)) * sz.cores + jnp.where(r >= 2 * sz.nx, 1, 0)
        held = dot(one_hot(c == source * sz.stride + sz.slots), x)
        lane = iota((128, sz.rows), 1)
        lane_place = lane - divided(lane, sz.stride, sz.rows) * sz.stride
        spread = one_hot(iota((128, sz.rows), 0) == lane_place)
        own = (block == source) & (
            jnp.where(is_txt, 1, 0) == jnp.where(place >= sz.cap, 1, 0)
        ) & (place < sz.slots)
        pool = jnp.zeros((count, sz.feat), f32)
        for part_at in range(3):
            piece = held[:, part_at * 128 : (part_at + 1) * 128].astype(bf16)
            weight = jnp.where(own, dot(piece, spread), 0.0).astype(bf16)
            pool = pool + dot(weight, out)
        me = lax.axis_index("expert")
        line = lax.axis_index("dp")
        my_x, my_core = me >> 1, me & 1
        row = iota((count, sz.feat), 0)
        my_row = my_core * (2 * sz.nx) + my_x
        pool = pool + jnp.where(row == my_row, means[0:1, :], 0.0)
        pool = pool + jnp.where(row == my_row + sz.nx, means[1:2, :], 0.0)
        lost = pool - pool.astype(bf16).astype(f32)
        img_lost = jnp.sum(jnp.where(row == my_row, lost, 0.0), axis=0, keepdims=True)
        txt_lost = jnp.sum(jnp.where(row == my_row + sz.nx, lost, 0.0), axis=0, keepdims=True)
        spare = iota((sz.stride, sz.feat), 0)
        blocks = []
        for e in range(sz.owners):
            kept = total[e * sz.stride : (e + 1) * sz.stride, :]
            kept = jnp.where(spare == sz.slots, img_lost, kept)
            blocks.append(jnp.where(spare == sz.slots + 1, txt_lost, kept))
            half = (e % sz.cores) * 2 * sz.nx
            blocks.append(pool[half : half + 2 * sz.nx, :])
        back_ref[...] = jnp.concatenate(blocks, 0).astype(bf16)
        r8 = iota((sz.nx, sz.rows), 0)
        c8 = iota((sz.nx, sz.rows), 1)
        labels = dot(one_hot(c8 == (r8 * sz.cores + my_core) * sz.stride + sz.slots + 1), x)
        lane = iota((sz.nx, sz.feat), 1)
        label_ref[...] = jnp.where((lane == line) | (lane == line + 128), labels, 0.0).astype(bf16)


def normalize_kernel(sz, back, label, out, copies):
    my_core = lax.axis_index("expert") & 1
    shape = (2 * sz.nx, sz.owners * sz.back)
    r, c = iota(shape, 0), iota(shape, 1)
    owner = divided(c, sz.back, shape[1])
    place = c - owner * sz.back
    spare = jnp.where(r >= sz.nx, sz.slots + 1, sz.slots)
    left = (place == spare) & (owner == (r & (sz.nx - 1)) * sz.cores + my_core)
    pooled = dot(one_hot((place == sz.stride + r) | left), back[...])
    norm = jnp.sqrt(jnp.sum(pooled * pooled, axis=1, keepdims=True) + 1e-06)
    block = jnp.concatenate([(pooled / norm).astype(bf16), label[...]], 0)
    out[...] = block
    for at in range(0, copies.shape[0], block.shape[0]):
        copies[at : at + block.shape[0], :] = block


def combine_kernel(sz, ie, ir, ik, te, tr, tk, ig, tg, img, txt, returned, img_out, txt_out):
    img_mask, txt_mask = slot_masks(sz, sz.back, ie[...], ir[...], ik[...], te[...], tr[...], tk[...])
    back = returned[...]
    for mask, gate, tokens, out in ((img_mask, ig, img, img_out), (txt_mask, tg, txt, txt_out)):
        count = tokens.shape[0]
        picked = dot(mask, back, TN)
        column = jnp.transpose(jnp.broadcast_to(gate[...], (128, count)))[:, 0:1]
        out[...] = (tokens[...].astype(f32) + column * picked).astype(bf16)


def merge_kernel(sz, got, copies):
    size = 3 * sz.nx
    count = got.shape[0] // size
    pieces = [got[b * size : b * size + sz.nx, :] for b in range(count)]
    pieces += [got[b * size + sz.nx : b * size + 2 * sz.nx, :] for b in range(count)]
    labels = jnp.zeros((sz.nx, sz.feat), f32)
    for b in range(count):
        labels = labels + got[b * size + 2 * sz.nx : (b + 1) * size, :].astype(f32)
    block = jnp.concatenate(pieces + [labels.astype(bf16)], 0)
    for at in range(0, copies.shape[0], block.shape[0]):
        copies[at : at + block.shape[0], :] = block


def head_kernel(sz, label_ref, own, mine, theirs, img_grad, txt_grad, images, texts):
    half = sz.half
    me = lax.axis_index("expert")
    line = lax.axis_index("dp")
    my_x, my_core = me >> 1, me & 1
    z_bits = sz.nz.bit_length() - 1
    pair = line * sz.owners + me

    def position(line, x, core):
        y, z = line >> z_bits, line & (sz.nz - 1)
        block = jnp.where(core == 0, z * sz.ny + y, y * sz.nz + z)
        return jnp.where(core == my_core, 0, half) + block * sz.nx + x

    blocks = sz.nz
    each = half // blocks
    size = 2 * each + sz.nx
    names = []
    for a, got in enumerate((mine, theirs)):
        table = jnp.zeros((sz.nx, 256), f32)
        for b in range(blocks):
            at, to = b * size, a * half + b * each
            images[to : to + each, :] = got[at : at + each, :]
            texts[to : to + each, :] = got[at + each : at + 2 * each, :]
            table = table + got[at + 2 * each : at + size, 0:256].astype(f32)
        names.append(table)

    total = 2 * half
    row_scores = jnp.exp(logit_scale * dot(own[: sz.nx, :], texts[...], NT))
    column_scores = jnp.exp(logit_scale * dot(images[...], own[sz.nx : 2 * sz.nx, :], NT))
    tile = min(256, total)
    column_totals = jnp.zeros((1, total), f32)
    row_totals = []
    for at in range(0, total, tile):
        scores = jnp.exp(logit_scale * dot(images[at : at + tile, :], texts[...], NT))
        row_totals.append(jnp.sum(scores, axis=1, keepdims=True))
        column_totals = column_totals + jnp.sum(scores, axis=0, keepdims=True)

    label = label_ref[0]
    owner = label & (sz.owners - 1)
    target = position(label >> (sz.owners.bit_length() - 1), owner >> 1, owner & 1)
    match = jnp.where(iota((sz.nx, total), 1) == target, 2.0, 0.0)
    own_rows = jnp.sum(row_scores, axis=1, keepdims=True)
    scores = row_scores / own_rows + row_scores / column_totals - match
    grad = dot(scores.astype(bf16), texts[...])
    chosen = iota((sz.nx, sz.feat), 0) == my_x
    img_grad[...] = jnp.sum(jnp.where(chosen, grad, 0.0), axis=0, keepdims=True)

    lane = iota((sz.nx, 128), 1)
    sub = iota((sz.nx, 128), 0)
    high, low = (pair >> 5).astype(f32), (pair & 31).astype(f32)
    found = []
    for table in names:
        hit = (table[:, :128] == high) & (table[:, 128:] == low) & (lane < sz.lines)

        def summed(value):
            value = jnp.where(hit, value, 0.0)
            return jnp.sum(jnp.sum(value, axis=0, keepdims=True), axis=1, keepdims=True)

        found.append([summed(v) for v in (lane.astype(f32), sub.astype(f32), jnp.ones((sz.nx, 128), f32))])
    found_line = (found[0][0] + found[1][0]).astype(i32)
    found_x = (found[0][1] + found[1][1]).astype(i32)
    found_core = jnp.where(found[1][2] > 0.5, 1 - my_core, my_core)
    named = position(found_line, found_x, found_core)
    own_columns = jnp.sum(column_scores, axis=0, keepdims=True)
    grad = jnp.zeros((sz.nx, sz.feat), f32)
    for t, at in enumerate(range(0, total, tile)):
        rows = column_scores[at : at + tile, :]
        match = jnp.where(iota((tile, sz.nx), 0) + at == named, 2.0, 0.0)
        scores = rows / row_totals[t] + rows / own_columns - match
        grad = grad + dot(scores.astype(bf16), images[at : at + tile, :], TN)
    txt_grad[...] = jnp.sum(jnp.where(chosen, grad, 0.0), axis=0, keepdims=True)


def call(kernel, out_shape, in_specs=None, cost=None, limit=24, **kw):
    if cost is not None:
        kw["cost_estimate"] = pl.CostEstimate(flops=cost[0], bytes_accessed=cost[1], transcendentals=cost[2])
    if in_specs is not None:
        kw["in_specs"] = in_specs
    return pl.pallas_call(
        kernel,
        out_shape=out_shape,
        compiler_params=pltpu.CompilerParams(vmem_limit_bytes=limit << 20),
        **kw,
    )


def bind(kernel, *head):
    def bound(*refs):
        return kernel(*head, *refs)

    return bound


def rank_of(sz, y, z, x, core):
    return ((y * sz.nz + z) * sz.nx + x) * sz.cores + core


def split_groups(sz, first):
    groups = []
    for core in range(sz.cores):
        along_y = (core == 0) == first
        for fixed in range(sz.nz if along_y else sz.ny):
            for x in range(sz.nx):
                if along_y:
                    groups.append([rank_of(sz, y, fixed, x, core) for y in range(sz.ny)])
                else:
                    groups.append([rank_of(sz, fixed, z, x, core) for z in range(sz.nz)])
    return groups


def per_device(
    image_tokens,
    text_tokens,
    text_counts,
    pair_labels,
    image_expert,
    image_rank,
    image_keep,
    text_expert,
    text_rank,
    text_keep,
    image_gate,
    text_gate,
    w_in,
    w_out,
):
    _, img_tok, feat = image_tokens.shape
    txt_tok = text_tokens.shape[1]
    sz = Sizes(lax.axis_size("expert"), lax.axis_size("dp"), img_tok, txt_tok, feat)
    ff = w_in.shape[2]
    img, txt = image_tokens[0], text_tokens[0]
    routes = (image_expert, image_rank, image_keep, text_expert, text_rank, text_keep)
    gates = (image_gate, text_gate)
    vmem = pl.BlockSpec(memory_space=pltpu.VMEM)
    smem = pl.BlockSpec(memory_space=pltpu.SMEM)

    def whole(shape):
        return pl.BlockSpec(shape, lambda i: (0, 0))

    packed, means = call(
        bind(dispatch_kernel, sz),
        (
            jax.ShapeDtypeStruct((sz.rows, feat), bf16),
            jax.ShapeDtypeStruct((8, feat), f32),
        ),
        grid=(1,),
        in_specs=[smem, smem]
        + [whole((1, img_tok))] * 3
        + [whole((1, txt_tok))] * 3
        + [whole((1, img_tok)), whole((1, txt_tok))]
        + [whole((img_tok, feat)), whole((txt_tok, feat))],
        out_specs=[whole((sz.rows, feat)), whole((8, feat))],
        limit=56,
        name="dispatch",
    )(text_counts, pair_labels, *routes, *gates, img, txt)

    def exchange(rows, count, axes="expert", groups=None):
        rows = rows.reshape(count, rows.shape[0] // count, feat)
        rows = lax.all_to_all(
            rows, axes, split_axis=0, concat_axis=0, tiled=True, axis_index_groups=groups
        )
        return rows.reshape(-1, feat)

    received = exchange(packed, sz.owners)
    block = min(512, ff)
    back_rows = sz.owners * sz.back
    rows, labels = call(
        bind(expert_kernel, sz, min(256, block)),
        (
            jax.ShapeDtypeStruct((back_rows, feat), bf16),
            jax.ShapeDtypeStruct((sz.nx, feat), bf16),
        ),
        grid=(ff // block,),
        in_specs=[
            whole((sz.rows, feat)),
            pl.BlockSpec((feat, block), lambda i: (0, i)),
            pl.BlockSpec((block, feat), lambda i: (i, 0)),
            whole((8, feat)),
        ],
        out_specs=[whole((back_rows, feat)), whole((sz.nx, feat))],
        scratch_shapes=[pltpu.VMEM((sz.rows, feat), f32)],
        limit=56,
        name="expert",
    )(received, w_in[0], w_out[0], means)
    returned = exchange(rows, sz.owners)

    size = 3 * sz.nx
    own, copies = call(
        bind(normalize_kernel, sz),
        (
            jax.ShapeDtypeStruct((size, feat), bf16),
            jax.ShapeDtypeStruct((sz.ny * size, feat), bf16),
        ),
        name="normalize",
    )(returned, labels)
    both = ("dp", "expert")
    got = exchange(copies, sz.ny, both, split_groups(sz, True))
    size = 2 * sz.ny * sz.nx + sz.nx
    copies = call(
        bind(merge_kernel, sz),
        jax.ShapeDtypeStruct((sz.nz * size, feat), bf16),
        name="merge",
    )(got)
    mine = exchange(copies, sz.nz, both, split_groups(sz, False))
    pairs = [(r, r ^ 1) for r in range(sz.pairs)]
    theirs = lax.ppermute(mine, both, pairs)
    img_out, txt_out = call(
        bind(combine_kernel, sz),
        (
            jax.ShapeDtypeStruct((img_tok, feat), bf16),
            jax.ShapeDtypeStruct((txt_tok, feat), bf16),
        ),
        cost=(2 * back_rows * (img_tok + txt_tok) * feat, 4 * back_rows * feat, 0),
        name="combine",
    )(*routes, *gates, img, txt, returned)
    img_grad, txt_grad = call(
        bind(head_kernel, sz),
        (
            jax.ShapeDtypeStruct((1, feat), f32),
            jax.ShapeDtypeStruct((1, feat), f32),
        ),
        in_specs=[smem] + [vmem] * 3,
        scratch_shapes=[pltpu.VMEM((sz.pairs, feat), bf16)] * 2,
        name="head",
    )(pair_labels, own, mine, theirs)
    return (img_out[None], txt_out[None], img_grad, txt_grad)


def solution(mesh):
    both = ("dp", "expert")
    return jax.shard_map(
        per_device,
        mesh=mesh,
        in_specs=(
            P(both, None, None),
            P(both, None, None),
            P(both),
            P(both),
            P(both, None),
            P(both, None),
            P(both, None),
            P(both, None),
            P(both, None),
            P(both, None),
            P(both, None),
            P(both, None),
            P("expert", None, None),
            P("expert", None, None),
        ),
        out_specs=(
            P(both, None, None),
            P(both, None, None),
            P(both, None),
            P(both, None),
        ),
        check_vma=False,
    )
```

```python
import jax
import jax.numpy as jnp
import numpy as np
from jax import lax
from jax.experimental import pallas as pl
from jax.experimental.pallas import tpu as pltpu
from jax.sharding import PartitionSpec as P

logit_scale = 10.0
f32, bf16, i32 = jnp.float32, jnp.bfloat16, jnp.int32
NT = (((1,), (1,)), ((), ()))
TN = (((0,), (0,)), ((), ()))
NN = (((1,), (0,)), ((), ()))


def dot(left, right, dims=NN):
    return lax.dot_general(left, right, dims, preferred_element_type=f32)


def divided(value, by, limit):
    magic = -(-65536 // by)
    assert all((v * magic) >> 16 == v // by for v in range(limit))
    return (value * magic) >> 16


def iota(shape, dim):
    return lax.broadcasted_iota(i32, shape, dim)


def one_hot(mask):
    return jnp.where(mask, 1.0, 0.0).astype(bf16)


def three_parts(value):
    high = value.astype(bf16)
    rest = value - high.astype(f32)
    middle = rest.astype(bf16)
    low = (rest - middle.astype(f32)).astype(bf16)
    return high, middle, low


class Sizes:
    def __init__(self, owners, lines, img_tok, txt_tok, feat):
        self.owners, self.lines = owners, lines
        self.cores = 2
        self.nx = owners // self.cores
        self.ny = 1 << ((lines.bit_length() - 1 + 1) // 2)
        self.nz = lines // self.ny
        self.img_tok, self.txt_tok, self.feat = img_tok, txt_tok, feat
        self.cap = 5 * img_tok // (4 * owners)
        self.slots = self.cap + 2
        self.stride = -(-(self.slots + 2) // 8) * 8
        self.rows = owners * self.stride
        self.per = self.nx // 2
        self.part = 2 * self.per
        self.back = self.stride + self.part
        self.half = self.nx * lines
        self.pairs = owners * lines


def slot_masks(sz, stride, img_expert, img_rank, img_keep, txt_expert, txt_rank, txt_keep):
    img_target = img_expert * stride + img_rank
    txt_target = txt_expert * stride + sz.cap + txt_rank
    img_target = jnp.where(img_keep == 1, img_target, -1)
    txt_target = jnp.where(txt_keep == 1, txt_target, -1)
    return (
        one_hot(iota((sz.owners * stride, sz.img_tok), 0) == img_target),
        one_hot(iota((sz.owners * stride, sz.txt_tok), 0) == txt_target),
    )


def dispatch_kernel(sz, count_ref, label_ref, *refs):
    sources, (packed, means, weights_ref) = refs[:11], refs[11:14]
    held, sems = refs[14:24], refs[24]
    copies = [
        pltpu.make_async_copy(source, target, sems.at[i])
        for i, (source, target) in enumerate(zip(sources, held + (weights_ref,)))
    ]
    for copy in copies:
        copy.start()
    for copy in copies[:10]:
        copy.wait()
    ie, ir, ik, te, tr, tk, ig, tg, img, txt = held
    img_mask, txt_mask = slot_masks(sz, sz.stride, ie[...], ir[...], ik[...], te[...], tr[...], tk[...])
    count = count_ref[0]
    count_f = jnp.full((1, 1), count, i32).astype(f32)
    label = label_ref[0]
    img_weight = jnp.where(ik[...] == 1, ig[...], 0.0) * (1.0 / sz.img_tok)
    valid = iota((1, sz.txt_tok), 1) < count
    txt_weight = jnp.where((tk[...] == 1) & valid, tg[...], 0.0) / count_f
    img_place = one_hot(iota((128, sz.img_tok), 0) == ir[...])
    txt_place = one_hot(iota((128, sz.txt_tok), 0) == tr[...] + sz.cap)
    img_at = iota((sz.owners, sz.img_tok), 0) == ie[...]
    txt_at = iota((sz.owners, sz.txt_tok), 0) == te[...]
    tables = []
    for img_part, txt_part in zip(three_parts(img_weight), three_parts(txt_weight)):
        img_side = jnp.where(img_at, img_part.astype(f32), 0.0).astype(bf16)
        txt_side = jnp.where(txt_at, txt_part.astype(f32), 0.0).astype(bf16)
        tables.append(dot(img_side, img_place, NT) + dot(txt_side, txt_place, NT))
    pad = sz.feat - 3 * 128
    if pad:
        tables.append(jnp.zeros((sz.owners, pad), f32))
    weights = jnp.concatenate(tables, 1).astype(bf16)
    lane = iota((sz.owners, sz.feat), 1)
    label_row = jnp.where(
        lane < 128,
        (label >> 5).astype(f32),
        jnp.where(lane < 256, (label & 31).astype(f32), 0.0),
    ).astype(bf16)
    row = iota((sz.rows, sz.owners), 0)
    block = iota((sz.rows, sz.owners), 1) * sz.stride
    out = dot(img_mask, img[...]) + dot(txt_mask, txt[...])
    out = out + dot(one_hot(row == block + sz.slots), weights)
    out = out + dot(one_hot(row == block + sz.slots + 1), label_row)
    packed[...] = out.astype(bf16)
    img_mean = dot(jnp.ones((8, sz.img_tok), bf16), img[...]) * (1.0 / sz.img_tok)
    counted = one_hot(iota((8, sz.txt_tok), 1) < count)
    txt_mean = dot(counted, txt[...]) / count_f
    means[...] = jnp.where(iota((8, sz.feat), 0) == 0, img_mean, txt_mean)
    copies[10].wait()


def source_of(sz, r):
    bits = sz.per.bit_length() - 1
    parity, core = (r >> (bits + 1)) & 1, r >> (bits + 2)
    return ((r & (sz.per - 1)) * 2 + parity) * sz.cores + core


def gelu(x):
    return 0.5 * x * (1.0 + lax.erf(x * np.float32(np.sqrt(0.5))))


def expert_kernel(sz, x_ref, w_in, w_out_source, means, back_ref, label_ref, w_out, sem):
    copy = pltpu.make_async_copy(w_out_source, w_out, sem)
    copy.start()
    x = x_ref[...]
    hidden = gelu(dot(x, w_in[...])).astype(bf16)
    copy.wait()
    total = dot(hidden, w_out[...])
    out = total.astype(bf16)
    me = lax.axis_index("expert")
    line = lax.axis_index("dp")
    my_x, my_core = me >> 1, me & 1
    count = 2 * sz.owners
    r = iota((count, sz.rows), 0)
    c = iota((count, sz.rows), 1)
    block = divided(c, sz.stride, sz.rows)
    place = c - block * sz.stride
    is_txt = r & sz.per
    source = source_of(sz, r)
    held = dot(one_hot(c == source * sz.stride + sz.slots), x)
    lane = iota((128, sz.rows), 1)
    lane_place = lane - divided(lane, sz.stride, sz.rows) * sz.stride
    spread = one_hot(iota((128, sz.rows), 0) == lane_place)
    own = (block == source) & (
        jnp.where(is_txt > 0, 1, 0) == jnp.where(place >= sz.cap, 1, 0)
    ) & (place < sz.slots)
    pool = jnp.zeros((count, sz.feat), f32)
    for part_at in range(3):
        piece = held[:, part_at * 128 : (part_at + 1) * 128].astype(bf16)
        weight = jnp.where(own, dot(piece, spread), 0.0).astype(bf16)
        pool = pool + dot(weight, out)
    row = iota((count, sz.feat), 0)
    my_row = (my_core * 2 + (my_x & 1)) * sz.part + (my_x >> 1)
    pool = pool + jnp.where(row == my_row, means[0:1, :], 0.0)
    pool = pool + jnp.where(row == my_row + sz.per, means[1:2, :], 0.0)
    lost = pool - pool.astype(bf16).astype(f32)
    img_lost = jnp.sum(jnp.where(row == my_row, lost, 0.0), axis=0, keepdims=True)
    txt_lost = jnp.sum(jnp.where(row == my_row + sz.per, lost, 0.0), axis=0, keepdims=True)
    spare = iota((sz.stride, sz.feat), 0)
    blocks = []
    for e in range(sz.owners):
        kept = total[e * sz.stride : (e + 1) * sz.stride, :]
        kept = jnp.where(spare == sz.slots, img_lost, kept)
        blocks.append(jnp.where(spare == sz.slots + 1, txt_lost, kept))
        group = (e % sz.cores) * 2 + (e // sz.cores) % 2
        blocks.append(pool[group * sz.part : (group + 1) * sz.part, :])
    back_ref[...] = jnp.concatenate(blocks, 0).astype(bf16)
    r8 = iota((sz.nx, sz.rows), 0)
    c8 = iota((sz.nx, sz.rows), 1)
    wanted = (c8 == (r8 * sz.cores + my_core) * sz.stride + sz.slots + 1) & ((r8 & 1) == (my_x & 1))
    labels = dot(one_hot(wanted), x)
    lane = iota((sz.nx, sz.feat), 1)
    label_ref[...] = jnp.where((lane == line) | (lane == line + 128), labels, 0.0).astype(bf16)


def normalize_kernel(sz, back, label, out, copies):
    me = lax.axis_index("expert")
    group = (me & 1) * 2 + ((me >> 1) & 1)
    shape = (sz.part, sz.owners * sz.back)
    r, c = iota(shape, 0), iota(shape, 1)
    owner = divided(c, sz.back, shape[1])
    place = c - owner * sz.back
    spare = jnp.where(r >= sz.per, sz.slots + 1, sz.slots)
    left = (place == spare) & (owner == source_of(sz, r + group * sz.part))
    pooled = dot(one_hot((place == sz.stride + r) | left), back[...])
    norm = jnp.sqrt(jnp.sum(pooled * pooled, axis=1, keepdims=True) + 1e-06)
    block = jnp.concatenate([(pooled / norm).astype(bf16), label[...]], 0)
    out[...] = block
    for at in range(0, copies.shape[0], block.shape[0]):
        copies[at : at + block.shape[0], :] = block


def combine_kernel(sz, ie, ir, ik, te, tr, tk, ig, tg, img, txt, returned, img_out, txt_out):
    img_mask, txt_mask = slot_masks(sz, sz.back, ie[...], ir[...], ik[...], te[...], tr[...], tk[...])
    back = returned[...]
    for mask, gate, tokens, out in ((img_mask, ig, img, img_out), (txt_mask, tg, txt, txt_out)):
        count = tokens.shape[0]
        picked = dot(mask, back, TN)
        column = jnp.transpose(jnp.broadcast_to(gate[...], (128, count)))[:, 0:1]
        out[...] = (tokens[...].astype(f32) + column * picked).astype(bf16)


def merge_kernel(sz, got, copies):
    size = sz.part + sz.nx
    members = got.shape[0] // size
    count = members * sz.per
    bits = sz.per.bit_length() - 1
    shape = (2 * count + sz.nx, got.shape[0])
    r, c = iota(shape, 0), iota(shape, 1)
    is_txt = jnp.where(r >= count, 1, 0)
    pair = r - is_txt * count
    place = (pair >> bits) * size + is_txt * sz.per + (pair & (sz.per - 1))
    is_label = r >= 2 * count
    label = (c & (size - 1)) == r - 2 * count + sz.part
    chosen = (is_label & label) | (jnp.logical_not(is_label) & (c == place))
    block = dot(one_hot(chosen), got[...]).astype(bf16)
    for at in range(0, copies.shape[0], block.shape[0]):
        copies[at : at + block.shape[0], :] = block


def head_kernel(sz, label_ref, own, mine, theirs, img_grad, txt_grad, images, texts):
    half = sz.half
    me = lax.axis_index("expert")
    line = lax.axis_index("dp")
    my_x, my_core = me >> 1, me & 1
    z_bits = sz.nz.bit_length() - 1
    pair = line * sz.owners + me

    def position(line, x, core):
        y, z = line >> z_bits, line & (sz.nz - 1)
        block = jnp.where(core == 0, z * sz.ny + y, y * sz.nz + z)
        place = (block * 2 + (x & 1)) * sz.per + (x >> 1)
        return jnp.where(core == my_core, 0, half) + place

    blocks = sz.nz
    each = half // blocks
    size = 2 * each + sz.nx
    names = []
    for a, got in enumerate((mine, theirs)):
        table = jnp.zeros((sz.nx, 256), f32)
        for b in range(blocks):
            at, to = b * size, a * half + b * each
            images[to : to + each, :] = got[at : at + each, :]
            texts[to : to + each, :] = got[at + each : at + 2 * each, :]
            table = table + got[at + 2 * each : at + size, 0:256].astype(f32)
        names.append(table)

    total = 2 * half
    near = own[: sz.part, :]
    row_scores = jnp.exp(logit_scale * dot(near, texts[...], NT))
    column_scores = jnp.exp(logit_scale * dot(images[...], near, NT))
    tile = min(256, total)
    column_totals = jnp.zeros((1, total), f32)
    row_totals = []
    for at in range(0, total, tile):
        scores = jnp.exp(logit_scale * dot(images[at : at + tile, :], texts[...], NT))
        row_totals.append(jnp.sum(scores, axis=1, keepdims=True))
        column_totals = column_totals + jnp.sum(scores, axis=0, keepdims=True)

    label = label_ref[0]
    owner = label & (sz.owners - 1)
    target = position(label >> (sz.owners.bit_length() - 1), owner >> 1, owner & 1)
    match = jnp.where(iota((sz.part, total), 1) == target, 2.0, 0.0)
    own_rows = jnp.sum(row_scores, axis=1, keepdims=True)
    scores = row_scores / own_rows + row_scores / column_totals - match
    grad = dot(scores.astype(bf16), texts[...])
    own_row = iota((sz.part, sz.feat), 0) - (my_x >> 1)
    img_grad[...] = jnp.sum(jnp.where(own_row == 0, grad, 0.0), axis=0, keepdims=True)

    lane = iota((sz.nx, 128), 1)
    sub = iota((sz.nx, 128), 0)
    high, low = (pair >> 5).astype(f32), (pair & 31).astype(f32)
    found = []
    for table in names:
        hit = (table[:, :128] == high) & (table[:, 128:] == low) & (lane < sz.lines)

        def summed(value):
            value = jnp.where(hit, value, 0.0)
            return jnp.sum(jnp.sum(value, axis=0, keepdims=True), axis=1, keepdims=True)

        found.append([summed(v) for v in (lane.astype(f32), sub.astype(f32), jnp.ones((sz.nx, 128), f32))])
    found_line = (found[0][0] + found[1][0]).astype(i32)
    found_x = (found[0][1] + found[1][1]).astype(i32)
    found_core = jnp.where(found[1][2] > 0.5, 1 - my_core, my_core)
    named = position(found_line, found_x, found_core)
    own_columns = jnp.sum(column_scores, axis=0, keepdims=True)
    grad = jnp.zeros((sz.part, sz.feat), f32)
    for t, at in enumerate(range(0, total, tile)):
        rows = column_scores[at : at + tile, :]
        match = jnp.where(iota((tile, sz.part), 0) + at == named, 2.0, 0.0)
        scores = rows / row_totals[t] + rows / own_columns - match
        grad = grad + dot(scores.astype(bf16), images[at : at + tile, :], TN)
    txt_grad[...] = jnp.sum(jnp.where(own_row == sz.per, grad, 0.0), axis=0, keepdims=True)


def call(kernel, out_shape, in_specs=None, cost=None, limit=24, **kw):
    if cost is not None:
        kw["cost_estimate"] = pl.CostEstimate(flops=cost[0], bytes_accessed=cost[1], transcendentals=cost[2])
    if in_specs is not None:
        kw["in_specs"] = in_specs
    return pl.pallas_call(
        kernel,
        out_shape=out_shape,
        compiler_params=pltpu.CompilerParams(vmem_limit_bytes=limit << 20),
        **kw,
    )


def bind(kernel, *head):
    def bound(*refs):
        return kernel(*head, *refs)

    return bound


def rank_of(sz, y, z, x, core):
    return ((y * sz.nz + z) * sz.nx + x) * sz.cores + core


def split_groups(sz, first):
    width = 2 if first else 1
    groups = []
    for core in range(sz.cores):
        along_y = (core == 0) == first
        for fixed in range(sz.nz if along_y else sz.ny):
            for x in range(0, sz.nx, width):
                group = []
                for moving in range(sz.ny if along_y else sz.nz):
                    y, z = (moving, fixed) if along_y else (fixed, moving)
                    group += [rank_of(sz, y, z, x + b, core) for b in range(width)]
                groups.append(group)
    return groups


def per_device(
    image_tokens,
    text_tokens,
    text_counts,
    pair_labels,
    image_expert,
    image_rank,
    image_keep,
    text_expert,
    text_rank,
    text_keep,
    image_gate,
    text_gate,
    w_in,
    w_out,
):
    _, img_tok, feat = image_tokens.shape
    txt_tok = text_tokens.shape[1]
    sz = Sizes(lax.axis_size("expert"), lax.axis_size("dp"), img_tok, txt_tok, feat)
    img, txt = image_tokens[0], text_tokens[0]
    routes = (image_expert, image_rank, image_keep, text_expert, text_rank, text_keep)
    gates = (image_gate, text_gate)
    vmem = pl.BlockSpec(memory_space=pltpu.VMEM)
    smem = pl.BlockSpec(memory_space=pltpu.SMEM)

    def whole(shape):
        return pl.BlockSpec(shape, lambda i: (0, 0))

    hbm = pl.BlockSpec(memory_space=pltpu.HBM)

    def in_hbm(value):
        return pltpu.with_memory_space_constraint(value, pltpu.HBM)

    ff = w_in.shape[2]
    counts, keys = (1, img_tok), (1, txt_tok)
    packed, means, w_in_held = call(
        bind(dispatch_kernel, sz),
        (
            jax.ShapeDtypeStruct((sz.rows, feat), bf16),
            jax.ShapeDtypeStruct((8, feat), f32),
            jax.ShapeDtypeStruct((feat, ff), bf16),
        ),
        in_specs=[smem, smem] + [hbm] * 11,
        out_specs=[vmem] * 3,
        scratch_shapes=[pltpu.VMEM(counts, i32)] * 3
        + [pltpu.VMEM(keys, i32)] * 3
        + [pltpu.VMEM(counts, f32), pltpu.VMEM(keys, f32)]
        + [pltpu.VMEM((img_tok, feat), bf16), pltpu.VMEM((txt_tok, feat), bf16)]
        + [pltpu.SemaphoreType.DMA((11,))],
        limit=16,
        name="dispatch",
    )(text_counts, pair_labels, *[in_hbm(v) for v in (*routes, *gates, img, txt, w_in[0])])

    def exchange(rows, count, axes="expert", groups=None):
        rows = rows.reshape(count, rows.shape[0] // count, feat)
        rows = lax.all_to_all(
            rows, axes, split_axis=0, concat_axis=0, tiled=True, axis_index_groups=groups
        )
        return rows.reshape(-1, feat)

    received = exchange(packed, sz.owners)
    back_rows = sz.owners * sz.back
    rows, labels = call(
        bind(expert_kernel, sz),
        (
            jax.ShapeDtypeStruct((back_rows, feat), bf16),
            jax.ShapeDtypeStruct((sz.nx, feat), bf16),
        ),
        in_specs=[vmem, vmem, hbm, vmem],
        scratch_shapes=[pltpu.VMEM((ff, feat), bf16), pltpu.SemaphoreType.DMA],
        limit=28,
        name="expert",
    )(received, w_in_held, w_out[0], means)
    returned = exchange(rows, sz.owners)

    size = sz.part + sz.nx
    own, copies = call(
        bind(normalize_kernel, sz),
        (
            jax.ShapeDtypeStruct((size, feat), bf16),
            jax.ShapeDtypeStruct((2 * sz.ny * size, feat), bf16),
        ),
        name="normalize",
    )(returned, labels)
    both = ("dp", "expert")
    got = exchange(copies, 2 * sz.ny, both, split_groups(sz, True))
    size = 2 * sz.ny * sz.nx + sz.nx
    copies = call(
        bind(merge_kernel, sz),
        jax.ShapeDtypeStruct((sz.nz * size, feat), bf16),
        name="merge",
    )(got)
    mine = exchange(copies, sz.nz, both, split_groups(sz, False))
    pairs = [(r, r ^ 1) for r in range(sz.pairs)]
    theirs = lax.ppermute(mine, both, pairs)
    img_out, txt_out = call(
        bind(combine_kernel, sz),
        (
            jax.ShapeDtypeStruct((img_tok, feat), bf16),
            jax.ShapeDtypeStruct((txt_tok, feat), bf16),
        ),
        cost=(2 * back_rows * (img_tok + txt_tok) * feat, 4 * back_rows * feat, 0),
        name="combine",
    )(*routes, *gates, img, txt, returned)
    img_grad, txt_grad = call(
        bind(head_kernel, sz),
        (
            jax.ShapeDtypeStruct((1, feat), f32),
            jax.ShapeDtypeStruct((1, feat), f32),
        ),
        in_specs=[smem] + [vmem] * 3,
        scratch_shapes=[pltpu.VMEM((sz.pairs, feat), bf16)] * 2,
        name="head",
    )(pair_labels, own, mine, theirs)
    return (img_out[None], txt_out[None], img_grad, txt_grad)


def solution(mesh):
    both = ("dp", "expert")
    return jax.shard_map(
        per_device,
        mesh=mesh,
        in_specs=(
            P(both, None, None),
            P(both, None, None),
            P(both),
            P(both),
            P(both, None),
            P(both, None),
            P(both, None),
            P(both, None),
            P(both, None),
            P(both, None),
            P(both, None),
            P(both, None),
            P("expert", None, None),
            P("expert", None, None),
        ),
        out_specs=(
            P(both, None, None),
            P(both, None, None),
            P(both, None),
            P(both, None),
        ),
        check_vma=False,
    )
```

```python
import jax
import jax.numpy as jnp
import numpy as np
from jax import lax
from jax.experimental import pallas as pl
from jax.experimental.pallas import tpu as pltpu
from jax.sharding import PartitionSpec as P

logit_scale = 10.0
f32, bf16, i32 = jnp.float32, jnp.bfloat16, jnp.int32
NT = (((1,), (1,)), ((), ()))
TN = (((0,), (0,)), ((), ()))
NN = (((1,), (0,)), ((), ()))


def dot(left, right, dims=NN):
    return lax.dot_general(left, right, dims, preferred_element_type=f32)


def divided(value, by, limit):
    magic = -(-65536 // by)
    assert all((v * magic) >> 16 == v // by for v in range(limit))
    return (value * magic) >> 16


def iota(shape, dim):
    return lax.broadcasted_iota(i32, shape, dim)


def one_hot(mask):
    return jnp.where(mask, 1.0, 0.0).astype(bf16)


def three_parts(value):
    high = value.astype(bf16)
    rest = value - high.astype(f32)
    middle = rest.astype(bf16)
    low = (rest - middle.astype(f32)).astype(bf16)
    return high, middle, low


class Sizes:
    def __init__(self, owners, lines, img_tok, txt_tok, feat):
        self.owners, self.lines = owners, lines
        self.cores = 2
        self.nx = owners // self.cores
        self.ny = 1 << ((lines.bit_length() - 1 + 1) // 2)
        self.nz = lines // self.ny
        self.img_tok, self.txt_tok, self.feat = img_tok, txt_tok, feat
        self.cap = 5 * img_tok // (4 * owners)
        self.slots = self.cap + 2
        self.stride = -(-(self.slots + 2) // 8) * 8
        self.rows = owners * self.stride
        self.per = self.nx // 2
        self.part = 2 * self.per
        self.back = self.stride + self.part
        self.half = self.nx * lines
        self.pairs = owners * lines


def slot_masks(sz, stride, img_expert, img_rank, img_keep, txt_expert, txt_rank, txt_keep):
    img_target = img_expert * stride + img_rank
    txt_target = txt_expert * stride + sz.cap + txt_rank
    img_target = jnp.where(img_keep == 1, img_target, -1)
    txt_target = jnp.where(txt_keep == 1, txt_target, -1)
    return (
        one_hot(iota((sz.owners * stride, sz.img_tok), 0) == img_target),
        one_hot(iota((sz.owners * stride, sz.txt_tok), 0) == txt_target),
    )


def dispatch_kernel(sz, count_ref, label_ref, *refs):
    sources, (packed, means, weights_ref) = refs[:11], refs[11:14]
    held, sems = refs[14:24], refs[24]
    copies = [
        pltpu.make_async_copy(source, target, sems.at[i])
        for i, (source, target) in enumerate(zip(sources, held + (weights_ref,)))
    ]
    for copy in copies:
        copy.start()
    for copy in copies[:10]:
        copy.wait()
    ie, ir, ik, te, tr, tk, ig, tg, img, txt = held
    img_mask, txt_mask = slot_masks(sz, sz.stride, ie[...], ir[...], ik[...], te[...], tr[...], tk[...])
    count, label = count_ref[0], label_ref[0]
    count_f = jnp.full((1, 1), count, i32).astype(f32)
    img_weight = jnp.where(ik[...] == 1, ig[...], 0.0) * (1.0 / sz.img_tok)
    valid = iota((1, sz.txt_tok), 1) < count
    txt_weight = jnp.where((tk[...] == 1) & valid, tg[...], 0.0) / count_f
    img_place = one_hot(iota((128, sz.img_tok), 0) == ir[...])
    txt_place = one_hot(iota((128, sz.txt_tok), 0) == tr[...] + sz.cap)
    img_at = iota((sz.owners, sz.img_tok), 0) == ie[...]
    txt_at = iota((sz.owners, sz.txt_tok), 0) == te[...]
    img_side = [jnp.where(img_at, part.astype(f32), 0.0) for part in three_parts(img_weight)]
    txt_side = [jnp.where(txt_at, part.astype(f32), 0.0) for part in three_parts(txt_weight)]
    table = dot(jnp.concatenate(img_side, 0).astype(bf16), img_place, NT)
    table = table + dot(jnp.concatenate(txt_side, 0).astype(bf16), txt_place, NT)
    tables = [table[at * sz.owners : (at + 1) * sz.owners] for at in range(3)]
    pad = sz.feat - 3 * 128
    if pad:
        tables.append(jnp.zeros((sz.owners, pad), f32))
    weights = jnp.concatenate(tables, 1).astype(bf16)
    lane = iota((sz.owners, sz.feat), 1)
    label_row = jnp.where(
        lane < 128,
        (label >> 5).astype(f32),
        jnp.where(lane < 256, (label & 31).astype(f32), 0.0),
    ).astype(bf16)
    row = iota((sz.rows, sz.owners), 0)
    block = iota((sz.rows, sz.owners), 1) * sz.stride
    out = dot(img_mask, img[...]) + dot(txt_mask, txt[...])
    out = out + dot(one_hot(row == block + sz.slots), weights)
    out = out + dot(one_hot(row == block + sz.slots + 1), label_row)
    packed[...] = out.astype(bf16)
    img_mean = dot(jnp.ones((8, sz.img_tok), bf16), img[...]) * (1.0 / sz.img_tok)
    counted = one_hot(iota((8, sz.txt_tok), 1) < count)
    txt_mean = dot(counted, txt[...]) / count_f
    means[...] = jnp.where(iota((8, sz.feat), 0) == 0, img_mean, txt_mean)
    copies[10].wait()


def source_of(sz, r):
    bits = sz.per.bit_length() - 1
    parity, core = (r >> (bits + 1)) & 1, r >> (bits + 2)
    return ((r & (sz.per - 1)) * 2 + parity) * sz.cores + core


def gelu(x):
    return 0.5 * x * (1.0 + lax.erf(x * np.float32(np.sqrt(0.5))))


def expert_kernel(sz, x_ref, w_in, w_out_source, means, back_ref, label_ref, w_out, sem):
    copy = pltpu.make_async_copy(w_out_source, w_out, sem)
    copy.start()
    x = x_ref[...]
    hidden = gelu(dot(x, w_in[...])).astype(bf16)
    copy.wait()
    total = dot(hidden, w_out[...])
    out = total.astype(bf16)
    me = lax.axis_index("expert")
    line = lax.axis_index("dp")
    my_x, my_core = me >> 1, me & 1
    count = 2 * sz.owners
    r = iota((count, sz.rows), 0)
    c = iota((count, sz.rows), 1)
    block = divided(c, sz.stride, sz.rows)
    place = c - block * sz.stride
    is_txt = r & sz.per
    source = source_of(sz, r)
    r8 = iota((sz.nx, sz.rows), 0)
    c8 = iota((sz.nx, sz.rows), 1)
    wanted = (c8 == (r8 * sz.cores + my_core) * sz.stride + sz.slots + 1) & ((r8 & 1) == (my_x & 1))
    weighing = jnp.where(c == source * sz.stride + sz.slots, 1.0, 0.0)
    labelling = jnp.where(wanted, 1.0, 0.0)
    held = dot(jnp.concatenate([weighing, labelling], 0).astype(bf16), x)
    labels = held[count:, :]
    lane = iota((128, sz.rows), 1)
    lane_place = lane - divided(lane, sz.stride, sz.rows) * sz.stride
    spread = one_hot(iota((128, sz.rows), 0) == lane_place)
    own = (block == source) & (
        jnp.where(is_txt > 0, 1, 0) == jnp.where(place >= sz.cap, 1, 0)
    ) & (place < sz.slots)
    pieces = [held[:count, at : at + 128] for at in (0, 128, 256)]
    weight = dot(jnp.concatenate(pieces, 0).astype(bf16), spread)
    weight = jnp.where(jnp.concatenate([own] * 3, 0), weight, 0.0)
    pool = dot(weight.astype(bf16), out)
    pool = pool[:count] + pool[count : 2 * count] + pool[2 * count :]
    row = iota((count, sz.feat), 0)
    my_row = (my_core * 2 + (my_x & 1)) * sz.part + (my_x >> 1)
    pool = pool + jnp.where(row == my_row, means[0:1, :], 0.0)
    pool = pool + jnp.where(row == my_row + sz.per, means[1:2, :], 0.0)
    lost = pool - pool.astype(bf16).astype(f32)
    img_lost = jnp.sum(jnp.where(row == my_row, lost, 0.0), axis=0, keepdims=True)
    txt_lost = jnp.sum(jnp.where(row == my_row + sz.per, lost, 0.0), axis=0, keepdims=True)
    spare = iota((sz.stride, sz.feat), 0)
    blocks = []
    for e in range(sz.owners):
        kept = total[e * sz.stride : (e + 1) * sz.stride, :]
        kept = jnp.where(spare == sz.slots, img_lost, kept)
        blocks.append(jnp.where(spare == sz.slots + 1, txt_lost, kept))
        group = (e % sz.cores) * 2 + (e // sz.cores) % 2
        blocks.append(pool[group * sz.part : (group + 1) * sz.part, :])
    back_ref[...] = jnp.concatenate(blocks, 0).astype(bf16)
    lane = iota((sz.nx, sz.feat), 1)
    label_ref[...] = jnp.where((lane == line) | (lane == line + 128), labels, 0.0).astype(bf16)


def normalize_kernel(sz, back, label, out, copies):
    me = lax.axis_index("expert")
    group = (me & 1) * 2 + ((me >> 1) & 1)
    shape = (sz.part, sz.owners * sz.back)
    r, c = iota(shape, 0), iota(shape, 1)
    owner = divided(c, sz.back, shape[1])
    place = c - owner * sz.back
    spare = jnp.where(r >= sz.per, sz.slots + 1, sz.slots)
    left = (place == spare) & (owner == source_of(sz, r + group * sz.part))
    pooled = dot(one_hot((place == sz.stride + r) | left), back[...])
    norm = jnp.sqrt(jnp.sum(pooled * pooled, axis=1, keepdims=True) + 1e-06)
    block = jnp.concatenate([(pooled / norm).astype(bf16), label[...]], 0)
    out[...] = block
    for at in range(0, copies.shape[0], block.shape[0]):
        copies[at : at + block.shape[0], :] = block


def combine_kernel(sz, ie, ir, ik, te, tr, tk, ig, tg, img, txt, returned, img_out, txt_out):
    img_mask, txt_mask = slot_masks(sz, sz.back, ie[...], ir[...], ik[...], te[...], tr[...], tk[...])
    back = returned[...]
    for mask, gate, tokens, out in ((img_mask, ig, img, img_out), (txt_mask, tg, txt, txt_out)):
        count = tokens.shape[0]
        picked = dot(mask, back, TN)
        column = jnp.transpose(jnp.broadcast_to(gate[...], (128, count)))[:, 0:1]
        out[...] = (tokens[...].astype(f32) + column * picked).astype(bf16)


def merge_kernel(sz, got, copies):
    size = sz.part + sz.nx
    members = got.shape[0] // size
    count = members * sz.per
    bits = sz.per.bit_length() - 1
    shape = (2 * count + sz.nx, got.shape[0])
    r, c = iota(shape, 0), iota(shape, 1)
    is_txt = jnp.where(r >= count, 1, 0)
    pair = r - is_txt * count
    place = (pair >> bits) * size + is_txt * sz.per + (pair & (sz.per - 1))
    is_label = r >= 2 * count
    label = (c & (size - 1)) == r - 2 * count + sz.part
    chosen = (is_label & label) | (jnp.logical_not(is_label) & (c == place))
    block = dot(one_hot(chosen), got[...]).astype(bf16)
    for at in range(0, copies.shape[0], block.shape[0]):
        copies[at : at + block.shape[0], :] = block


def unpack(sz, got, images, texts):
    each = sz.half // sz.nz
    size = 2 * each + sz.nx
    table = jnp.zeros((sz.nx, 256), f32)
    for b in range(sz.nz):
        at, to = b * size, b * each
        images[to : to + each, :] = got[at : at + each, :]
        texts[to : to + each, :] = got[at + each : at + 2 * each, :]
        table = table + got[at + 2 * each : at + size, 0:256].astype(f32)
    return table


def exp_scores(left, right):
    return jnp.exp(logit_scale * dot(left, right, NT))


def first_head_kernel(sz, own, mine, images, texts, table, row_totals, column_totals, strips):
    half = sz.half
    table[...] = unpack(sz, mine, images, texts)
    tile = min(256, half)
    totals = jnp.zeros((1, half), f32)
    for at in range(0, half, tile):
        scores = exp_scores(images[at : at + tile, :], texts[...])
        row_totals[at : at + tile, :] = jnp.sum(scores, axis=1, keepdims=True)
        totals = totals + jnp.sum(scores, axis=0, keepdims=True)
    column_totals[...] = totals
    strips[...] = exp_scores(own[: sz.part, :], texts[...])


def head_kernel(
    sz, label_ref, own, theirs, images_a, texts_a, table_a, rows_a, columns_a, strip_a,
    img_grad, txt_grad, images_b, texts_b,
):
    half = sz.half
    me = lax.axis_index("expert")
    line = lax.axis_index("dp")
    my_x, my_core = me >> 1, me & 1
    z_bits = sz.nz.bit_length() - 1
    pair = line * sz.owners + me

    def position(line, x, core):
        y, z = line >> z_bits, line & (sz.nz - 1)
        block = jnp.where(core == 0, z * sz.ny + y, y * sz.nz + z)
        place = (block * 2 + (x & 1)) * sz.per + (x >> 1)
        return jnp.where(core == my_core, 0, half) + place

    names = [table_a[...], unpack(sz, theirs, images_b, texts_b)]
    near = own[: sz.part, :]
    tile = min(256, half)
    columns = [columns_a[...], jnp.zeros((1, half), f32)]
    rows = [[rows_a[at : at + tile, :] for at in range(0, half, tile)], []]
    for t, at in enumerate(range(0, half, tile)):
        scores = exp_scores(images_a[at : at + tile, :], texts_b[...])
        rows[0][t] = rows[0][t] + jnp.sum(scores, axis=1, keepdims=True)
        columns[1] = columns[1] + jnp.sum(scores, axis=0, keepdims=True)
    for at in range(0, half, tile):
        total = jnp.zeros((tile, 1), f32)
        for b, texts in enumerate((texts_a, texts_b)):
            scores = exp_scores(images_b[at : at + tile, :], texts[...])
            total = total + jnp.sum(scores, axis=1, keepdims=True)
            columns[b] = columns[b] + jnp.sum(scores, axis=0, keepdims=True)
        rows[1].append(total)

    label = label_ref[0]
    owner = label & (sz.owners - 1)
    target = position(label >> (sz.owners.bit_length() - 1), owner >> 1, owner & 1)
    strips = [strip_a[...], exp_scores(near, texts_b[...])]
    own_rows = sum(jnp.sum(strip, axis=1, keepdims=True) for strip in strips)
    grad = jnp.zeros((sz.part, sz.feat), f32)
    for b, texts in enumerate((texts_a, texts_b)):
        match = jnp.where(iota((sz.part, half), 1) + b * half == target, 2.0, 0.0)
        scores = strips[b] / own_rows + strips[b] / columns[b] - match
        grad = grad + dot(scores.astype(bf16), texts[...])
    own_row = iota((sz.part, sz.feat), 0) - (my_x >> 1)
    img_grad[...] = jnp.sum(jnp.where(own_row == 0, grad, 0.0), axis=0, keepdims=True)

    lane = iota((sz.nx, 128), 1)
    sub = iota((sz.nx, 128), 0)
    high, low = (pair >> 5).astype(f32), (pair & 31).astype(f32)
    found = []
    for table in names:
        hit = (table[:, :128] == high) & (table[:, 128:] == low) & (lane < sz.lines)

        def summed(value):
            value = jnp.where(hit, value, 0.0)
            return jnp.sum(jnp.sum(value, axis=0, keepdims=True), axis=1, keepdims=True)

        found.append([summed(v) for v in (lane.astype(f32), sub.astype(f32), jnp.ones((sz.nx, 128), f32))])
    found_line = (found[0][0] + found[1][0]).astype(i32)
    found_x = (found[0][1] + found[1][1]).astype(i32)
    found_core = jnp.where(found[1][2] > 0.5, 1 - my_core, my_core)
    named = position(found_line, found_x, found_core)
    strips = [exp_scores(images[...], near) for images in (images_a, images_b)]
    own_columns = sum(jnp.sum(strip, axis=0, keepdims=True) for strip in strips)
    grad = jnp.zeros((sz.part, sz.feat), f32)
    for a, images in enumerate((images_a, images_b)):
        for t, at in enumerate(range(0, half, tile)):
            strip = strips[a][at : at + tile, :]
            match = jnp.where(iota((tile, sz.part), 0) + a * half + at == named, 2.0, 0.0)
            scores = strip / rows[a][t] + strip / own_columns - match
            grad = grad + dot(scores.astype(bf16), images[at : at + tile, :], TN)
    txt_grad[...] = jnp.sum(jnp.where(own_row == sz.per, grad, 0.0), axis=0, keepdims=True)


def call(kernel, out_shape, in_specs=None, cost=None, limit=24, **kw):
    if cost is not None:
        kw["cost_estimate"] = pl.CostEstimate(flops=cost[0], bytes_accessed=cost[1], transcendentals=cost[2])
    if in_specs is not None:
        kw["in_specs"] = in_specs
    return pl.pallas_call(
        kernel,
        out_shape=out_shape,
        compiler_params=pltpu.CompilerParams(vmem_limit_bytes=limit << 20),
        **kw,
    )


def bind(kernel, *head):
    def bound(*refs):
        return kernel(*head, *refs)

    return bound


def rank_of(sz, y, z, x, core):
    return ((y * sz.nz + z) * sz.nx + x) * sz.cores + core


def split_groups(sz, first):
    width = 2 if first else 1
    groups = []
    for core in range(sz.cores):
        along_y = (core == 0) == first
        for fixed in range(sz.nz if along_y else sz.ny):
            for x in range(0, sz.nx, width):
                group = []
                for moving in range(sz.ny if along_y else sz.nz):
                    y, z = (moving, fixed) if along_y else (fixed, moving)
                    group += [rank_of(sz, y, z, x + b, core) for b in range(width)]
                groups.append(group)
    return groups


def per_device(
    image_tokens,
    text_tokens,
    text_counts,
    pair_labels,
    image_expert,
    image_rank,
    image_keep,
    text_expert,
    text_rank,
    text_keep,
    image_gate,
    text_gate,
    w_in,
    w_out,
):
    _, img_tok, feat = image_tokens.shape
    txt_tok = text_tokens.shape[1]
    sz = Sizes(lax.axis_size("expert"), lax.axis_size("dp"), img_tok, txt_tok, feat)
    img, txt = image_tokens[0], text_tokens[0]
    routes = (image_expert, image_rank, image_keep, text_expert, text_rank, text_keep)
    gates = (image_gate, text_gate)
    vmem = pl.BlockSpec(memory_space=pltpu.VMEM)
    smem = pl.BlockSpec(memory_space=pltpu.SMEM)

    def whole(shape):
        return pl.BlockSpec(shape, lambda i: (0, 0))

    hbm = pl.BlockSpec(memory_space=pltpu.HBM)

    def in_hbm(value):
        return pltpu.with_memory_space_constraint(value, pltpu.HBM)

    ff = w_in.shape[2]
    counts, keys = (1, img_tok), (1, txt_tok)
    packed, means, w_in_held = call(
        bind(dispatch_kernel, sz),
        (
            jax.ShapeDtypeStruct((sz.rows, feat), bf16),
            jax.ShapeDtypeStruct((8, feat), f32),
            jax.ShapeDtypeStruct((feat, ff), bf16),
        ),
        in_specs=[smem] * 2 + [hbm] * 11,
        out_specs=[vmem] * 3,
        scratch_shapes=[pltpu.VMEM(counts, i32)] * 3
        + [pltpu.VMEM(keys, i32)] * 3
        + [pltpu.VMEM(counts, f32), pltpu.VMEM(keys, f32)]
        + [pltpu.VMEM((img_tok, feat), bf16), pltpu.VMEM((txt_tok, feat), bf16)]
        + [pltpu.SemaphoreType.DMA((11,))],
        limit=16,
        name="dispatch",
    )(text_counts, pair_labels, *[in_hbm(v) for v in (*routes, *gates, img, txt, w_in[0])])

    def exchange(rows, count, axes="expert", groups=None):
        rows = rows.reshape(count, rows.shape[0] // count, feat)
        rows = lax.all_to_all(
            rows, axes, split_axis=0, concat_axis=0, tiled=True, axis_index_groups=groups
        )
        return rows.reshape(-1, feat)

    received = exchange(packed, sz.owners)
    back_rows = sz.owners * sz.back
    rows, labels = call(
        bind(expert_kernel, sz),
        (
            jax.ShapeDtypeStruct((back_rows, feat), bf16),
            jax.ShapeDtypeStruct((sz.nx, feat), bf16),
        ),
        in_specs=[vmem, vmem, hbm, vmem],
        scratch_shapes=[pltpu.VMEM((ff, feat), bf16), pltpu.SemaphoreType.DMA],
        limit=28,
        name="expert",
    )(received, w_in_held, w_out[0], means)
    returned = exchange(rows, sz.owners)

    size = sz.part + sz.nx
    own, copies = call(
        bind(normalize_kernel, sz),
        (
            jax.ShapeDtypeStruct((size, feat), bf16),
            jax.ShapeDtypeStruct((2 * sz.ny * size, feat), bf16),
        ),
        name="normalize",
    )(returned, labels)
    both = ("dp", "expert")
    got = exchange(copies, 2 * sz.ny, both, split_groups(sz, True))
    size = 2 * sz.ny * sz.nx + sz.nx
    copies = call(
        bind(merge_kernel, sz),
        jax.ShapeDtypeStruct((sz.nz * size, feat), bf16),
        name="merge",
    )(got)
    mine = exchange(copies, sz.nz, both, split_groups(sz, False))
    pairs = [(r, r ^ 1) for r in range(sz.pairs)]
    theirs = lax.ppermute(mine, both, pairs)
    img_out, txt_out = call(
        bind(combine_kernel, sz),
        (
            jax.ShapeDtypeStruct((img_tok, feat), bf16),
            jax.ShapeDtypeStruct((txt_tok, feat), bf16),
        ),
        cost=(2 * back_rows * (img_tok + txt_tok) * feat, 4 * back_rows * feat, 0),
        name="combine",
    )(*routes, *gates, img, txt, returned)
    halves = [jax.ShapeDtypeStruct((sz.half, feat), bf16)] * 2
    first = call(
        bind(first_head_kernel, sz),
        (
            *halves,
            jax.ShapeDtypeStruct((sz.nx, 256), f32),
            jax.ShapeDtypeStruct((sz.half, 1), f32),
            jax.ShapeDtypeStruct((1, sz.half), f32),
            jax.ShapeDtypeStruct((sz.part, sz.half), f32),
        ),
        cost=(2 * sz.half * sz.half * feat, 4 * sz.half * feat, sz.half * sz.half),
        name="first_head",
    )(own, mine)
    img_grad, txt_grad = call(
        bind(head_kernel, sz),
        (
            jax.ShapeDtypeStruct((1, feat), f32),
            jax.ShapeDtypeStruct((1, feat), f32),
        ),
        in_specs=[smem] + [vmem] * 8,
        scratch_shapes=[pltpu.VMEM((sz.half, feat), bf16)] * 2,
        name="head",
    )(pair_labels, own, theirs, *first)
    return (img_out[None], txt_out[None], img_grad, txt_grad)


def solution(mesh):
    both = ("dp", "expert")
    return jax.shard_map(
        per_device,
        mesh=mesh,
        in_specs=(
            P(both, None, None),
            P(both, None, None),
            P(both),
            P(both),
            P(both, None),
            P(both, None),
            P(both, None),
            P(both, None),
            P(both, None),
            P(both, None),
            P(both, None),
            P(both, None),
            P("expert", None, None),
            P("expert", None, None),
        ),
        out_specs=(
            P(both, None, None),
            P(both, None, None),
            P(both, None),
            P(both, None),
        ),
        check_vma=False,
    )
```

```python
import jax
import jax.numpy as jnp
import numpy as np
from jax import lax
from jax.experimental import pallas as pl
from jax.experimental.pallas import tpu as pltpu
from jax.sharding import PartitionSpec as P

logit_scale = 10.0
f32, bf16, i32 = jnp.float32, jnp.bfloat16, jnp.int32
NT = (((1,), (1,)), ((), ()))
TN = (((0,), (0,)), ((), ()))
NN = (((1,), (0,)), ((), ()))


def dot(left, right, dims=NN):
    return lax.dot_general(left, right, dims, preferred_element_type=f32)


def divided(value, by, limit):
    magic = -(-65536 // by)
    assert all((v * magic) >> 16 == v // by for v in range(limit))
    return (value * magic) >> 16


def iota(shape, dim):
    return lax.broadcasted_iota(i32, shape, dim)


def one_hot(mask):
    return jnp.where(mask, 1.0, 0.0).astype(bf16)


def three_parts(value):
    high = value.astype(bf16)
    rest = value - high.astype(f32)
    middle = rest.astype(bf16)
    low = (rest - middle.astype(f32)).astype(bf16)
    return high, middle, low


class Sizes:
    def __init__(self, owners, lines, img_tok, txt_tok, feat):
        self.owners, self.lines = owners, lines
        self.cores = 2
        self.nx = owners // self.cores
        self.ny = 1 << ((lines.bit_length() - 1 + 1) // 2)
        self.nz = lines // self.ny
        self.img_tok, self.txt_tok, self.feat = img_tok, txt_tok, feat
        self.cap = 5 * img_tok // (4 * owners)
        self.slots = self.cap + 2
        self.stride = -(-(self.slots + 2) // 8) * 8
        self.rows = owners * self.stride
        self.per = self.nx // 2
        self.part = 2 * self.per
        self.back = self.stride + self.part
        self.half = self.nx * lines
        self.pairs = owners * lines


def slot_masks(sz, stride, img_expert, img_rank, img_keep, txt_expert, txt_rank, txt_keep):
    img_target = img_expert * stride + img_rank
    txt_target = txt_expert * stride + sz.cap + txt_rank
    img_target = jnp.where(img_keep == 1, img_target, -1)
    txt_target = jnp.where(txt_keep == 1, txt_target, -1)
    return (
        one_hot(iota((sz.owners * stride, sz.img_tok), 0) == img_target),
        one_hot(iota((sz.owners * stride, sz.txt_tok), 0) == txt_target),
    )


def dispatch_kernel(sz, count_ref, label_ref, *refs):
    sources, (packed, means, weights_ref) = refs[:11], refs[11:14]
    held, sems = refs[14:24], refs[24]
    copies = [
        pltpu.make_async_copy(source, target, sems.at[i])
        for i, (source, target) in enumerate(zip(sources, held + (weights_ref,)))
    ]
    for copy in copies:
        copy.start()
    for copy in copies[:10]:
        copy.wait()
    ie, ir, ik, te, tr, tk, ig, tg, img, txt = held
    img_mask, txt_mask = slot_masks(sz, sz.stride, ie[...], ir[...], ik[...], te[...], tr[...], tk[...])
    count, label = count_ref[0], label_ref[0]
    count_f = jnp.full((1, 1), count, i32).astype(f32)
    img_weight = jnp.where(ik[...] == 1, ig[...], 0.0) * (1.0 / sz.img_tok)
    valid = iota((1, sz.txt_tok), 1) < count
    txt_weight = jnp.where((tk[...] == 1) & valid, tg[...], 0.0) / count_f
    img_place = one_hot(iota((128, sz.img_tok), 0) == ir[...])
    txt_place = one_hot(iota((128, sz.txt_tok), 0) == tr[...] + sz.cap)
    img_at = iota((sz.owners, sz.img_tok), 0) == ie[...]
    txt_at = iota((sz.owners, sz.txt_tok), 0) == te[...]
    img_side = [jnp.where(img_at, part.astype(f32), 0.0) for part in three_parts(img_weight)]
    txt_side = [jnp.where(txt_at, part.astype(f32), 0.0) for part in three_parts(txt_weight)]
    table = dot(jnp.concatenate(img_side, 0).astype(bf16), img_place, NT)
    table = table + dot(jnp.concatenate(txt_side, 0).astype(bf16), txt_place, NT)
    tables = [table[at * sz.owners : (at + 1) * sz.owners] for at in range(3)]
    pad = sz.feat - 3 * 128
    if pad:
        tables.append(jnp.zeros((sz.owners, pad), f32))
    weights = jnp.concatenate(tables, 1).astype(bf16)
    lane = iota((sz.owners, sz.feat), 1)
    label_row = jnp.where(
        lane < 128,
        (label >> 5).astype(f32),
        jnp.where(lane < 256, (label & 31).astype(f32), 0.0),
    ).astype(bf16)
    row = iota((sz.rows, sz.owners), 0)
    block = iota((sz.rows, sz.owners), 1) * sz.stride
    out = dot(img_mask, img[...]) + dot(txt_mask, txt[...])
    out = out + dot(one_hot(row == block + sz.slots), weights)
    out = out + dot(one_hot(row == block + sz.slots + 1), label_row)
    packed[...] = out.astype(bf16)
    img_mean = dot(jnp.ones((8, sz.img_tok), bf16), img[...]) * (1.0 / sz.img_tok)
    counted = one_hot(iota((8, sz.txt_tok), 1) < count)
    txt_mean = dot(counted, txt[...]) / count_f
    means[...] = jnp.where(iota((8, sz.feat), 0) == 0, img_mean, txt_mean)
    copies[10].wait()


def source_of(sz, r):
    bits = sz.per.bit_length() - 1
    parity, core = (r >> (bits + 1)) & 1, r >> (bits + 2)
    return ((r & (sz.per - 1)) * 2 + parity) * sz.cores + core


def gelu(x):
    return 0.5 * x * (1.0 + lax.erf(x * np.float32(np.sqrt(0.5))))


def expert_kernel(sz, x_ref, w_in, w_out_source, means, back_ref, label_ref, w_out, sem):
    copy = pltpu.make_async_copy(w_out_source, w_out, sem)
    copy.start()
    x = x_ref[...]
    hidden = gelu(dot(x, w_in[...])).astype(bf16)
    copy.wait()
    total = dot(hidden, w_out[...])
    out = total.astype(bf16)
    me = lax.axis_index("expert")
    line = lax.axis_index("dp")
    my_x, my_core = me >> 1, me & 1
    count = 2 * sz.owners
    r = iota((count, sz.rows), 0)
    c = iota((count, sz.rows), 1)
    block = divided(c, sz.stride, sz.rows)
    place = c - block * sz.stride
    is_txt = r & sz.per
    source = source_of(sz, r)
    r8 = iota((sz.part, sz.rows), 0)
    c8 = iota((sz.part, sz.rows), 1)
    named = (r8 * 2 + (my_x & 1)) * sz.cores + my_core
    wanted = (c8 == named * sz.stride + sz.slots + 1) & (r8 < sz.per)
    weighing = jnp.where(c == source * sz.stride + sz.slots, 1.0, 0.0)
    labelling = jnp.where(wanted, 1.0, 0.0)
    held = dot(jnp.concatenate([weighing, labelling], 0).astype(bf16), x)
    labels = held[count:, :]
    lane = iota((128, sz.rows), 1)
    lane_place = lane - divided(lane, sz.stride, sz.rows) * sz.stride
    spread = one_hot(iota((128, sz.rows), 0) == lane_place)
    own = (block == source) & (
        jnp.where(is_txt > 0, 1, 0) == jnp.where(place >= sz.cap, 1, 0)
    ) & (place < sz.slots)
    pieces = [held[:count, at : at + 128] for at in (0, 128, 256)]
    weight = dot(jnp.concatenate(pieces, 0).astype(bf16), spread)
    weight = jnp.where(jnp.concatenate([own] * 3, 0), weight, 0.0)
    pool = dot(weight.astype(bf16), out)
    pool = pool[:count] + pool[count : 2 * count] + pool[2 * count :]
    row = iota((count, sz.feat), 0)
    my_row = (my_core * 2 + (my_x & 1)) * sz.part + (my_x >> 1)
    pool = pool + jnp.where(row == my_row, means[0:1, :], 0.0)
    pool = pool + jnp.where(row == my_row + sz.per, means[1:2, :], 0.0)
    lost = pool - pool.astype(bf16).astype(f32)
    img_lost = jnp.sum(jnp.where(row == my_row, lost, 0.0), axis=0, keepdims=True)
    txt_lost = jnp.sum(jnp.where(row == my_row + sz.per, lost, 0.0), axis=0, keepdims=True)
    spare = iota((sz.stride, sz.feat), 0)
    blocks = []
    for e in range(sz.owners):
        kept = total[e * sz.stride : (e + 1) * sz.stride, :]
        kept = jnp.where(spare == sz.slots, img_lost, kept)
        blocks.append(jnp.where(spare == sz.slots + 1, txt_lost, kept))
        group = (e % sz.cores) * 2 + (e // sz.cores) % 2
        blocks.append(pool[group * sz.part : (group + 1) * sz.part, :])
    back_ref[...] = jnp.concatenate(blocks, 0).astype(bf16)
    lane = iota((sz.part, 128), 1)
    low = jnp.where(lane == line + 64, labels[:, 128:256], 0.0)
    label_ref[...] = jnp.where(lane == line, labels[:, :128], low).astype(bf16)


def normalize_kernel(sz, back, label, out, copies):
    me = lax.axis_index("expert")
    group = (me & 1) * 2 + ((me >> 1) & 1)
    shape = (sz.part, sz.owners * sz.back)
    r, c = iota(shape, 0), iota(shape, 1)
    owner = divided(c, sz.back, shape[1])
    place = c - owner * sz.back
    spare = jnp.where(r >= sz.per, sz.slots + 1, sz.slots)
    left = (place == spare) & (owner == source_of(sz, r + group * sz.part))
    pooled = dot(one_hot((place == sz.stride + r) | left), back[...])
    norm = jnp.sqrt(jnp.sum(pooled * pooled, axis=1, keepdims=True) + 1e-06)
    out[...] = (pooled / norm).astype(bf16)
    block = jnp.concatenate([out[...], label[...]], 1)
    for at in range(0, copies.shape[0], block.shape[0]):
        copies[at : at + block.shape[0], :] = block


def combine_kernel(sz, ie, ir, ik, te, tr, tk, ig, tg, img, txt, returned, img_out, txt_out):
    img_mask, txt_mask = slot_masks(sz, sz.back, ie[...], ir[...], ik[...], te[...], tr[...], tk[...])
    back = returned[...]
    for mask, gate, tokens, out in ((img_mask, ig, img, img_out), (txt_mask, tg, txt, txt_out)):
        count = tokens.shape[0]
        picked = dot(mask, back, TN)
        column = jnp.transpose(jnp.broadcast_to(gate[...], (128, count)))[:, 0:1]
        out[...] = (tokens[...].astype(f32) + column * picked).astype(bf16)


def merge_kernel(sz, got, copies):
    size = sz.part
    members = got.shape[0] // size
    count = members * sz.per
    bits = sz.per.bit_length() - 1
    shape = (2 * count + sz.nx, got.shape[0])
    r, c = iota(shape, 0), iota(shape, 1)
    is_txt = jnp.where(r >= count, 1, 0)
    pair = r - is_txt * count
    place = (pair >> bits) * size + is_txt * sz.per + (pair & (sz.per - 1))
    x = r - 2 * count
    label = ((c & (size - 1)) == (x >> 1)) & (((c >> (bits + 1)) & 1) == (x & 1))
    chosen = ((r >= 2 * count) & label) | ((r < 2 * count) & (c == place))
    all_rows = dot(one_hot(chosen), got[...]).astype(bf16)
    labels = all_rows[2 * count :, sz.feat :]
    padding = jnp.zeros((sz.nx, sz.feat - 128), bf16)
    block = jnp.concatenate(
        [all_rows[: 2 * count, : sz.feat], jnp.concatenate([labels, padding], 1)], 0
    )
    for at in range(0, copies.shape[0], block.shape[0]):
        copies[at : at + block.shape[0], :] = block


def unpack(sz, got, images, texts):
    each = sz.half // sz.nz
    size = 2 * each + sz.nx
    table = jnp.zeros((sz.nx, 128), f32)
    for b in range(sz.nz):
        at, to = b * size, b * each
        images[to : to + each, :] = got[at : at + each, :]
        texts[to : to + each, :] = got[at + each : at + 2 * each, :]
        table = table + got[at + 2 * each : at + size, 0:128].astype(f32)
    return table


def exp_scores(left, right):
    return jnp.exp(logit_scale * dot(left, right, NT))


def first_head_kernel(sz, own, mine, images, texts, table, row_totals, column_totals, strips):
    half = sz.half
    table[...] = unpack(sz, mine, images, texts)
    tile = min(256, half)
    totals = jnp.zeros((1, half), f32)
    for at in range(0, half, tile):
        scores = exp_scores(images[at : at + tile, :], texts[...])
        row_totals[at : at + tile, :] = jnp.sum(scores, axis=1, keepdims=True)
        totals = totals + jnp.sum(scores, axis=0, keepdims=True)
    column_totals[...] = totals
    strips[...] = exp_scores(own[...], texts[...])


def head_kernel(
    sz, label_ref, own, theirs, images_a, texts_a, table_a, rows_a, columns_a, strip_a,
    img_grad, txt_grad, images_b, texts_b,
):
    half = sz.half
    me = lax.axis_index("expert")
    line = lax.axis_index("dp")
    my_x, my_core = me >> 1, me & 1
    z_bits = sz.nz.bit_length() - 1
    pair = line * sz.owners + me

    def position(line, x, core):
        y, z = line >> z_bits, line & (sz.nz - 1)
        block = jnp.where(core == 0, z * sz.ny + y, y * sz.nz + z)
        place = (block * 2 + (x & 1)) * sz.per + (x >> 1)
        return jnp.where(core == my_core, 0, half) + place

    names = [table_a[...], unpack(sz, theirs, images_b, texts_b)]
    near = own[...]
    tile = min(256, half)
    columns = [columns_a[...], jnp.zeros((1, half), f32)]
    rows = [[rows_a[at : at + tile, :] for at in range(0, half, tile)], []]
    for t, at in enumerate(range(0, half, tile)):
        scores = exp_scores(images_a[at : at + tile, :], texts_b[...])
        rows[0][t] = rows[0][t] + jnp.sum(scores, axis=1, keepdims=True)
        columns[1] = columns[1] + jnp.sum(scores, axis=0, keepdims=True)
    for at in range(0, half, tile):
        total = jnp.zeros((tile, 1), f32)
        for b, texts in enumerate((texts_a, texts_b)):
            scores = exp_scores(images_b[at : at + tile, :], texts[...])
            total = total + jnp.sum(scores, axis=1, keepdims=True)
            columns[b] = columns[b] + jnp.sum(scores, axis=0, keepdims=True)
        rows[1].append(total)

    label = label_ref[0]
    owner = label & (sz.owners - 1)
    target = position(label >> (sz.owners.bit_length() - 1), owner >> 1, owner & 1)
    strips = [strip_a[...], exp_scores(near, texts_b[...])]
    own_rows = sum(jnp.sum(strip, axis=1, keepdims=True) for strip in strips)
    grad = jnp.zeros((sz.part, sz.feat), f32)
    for b, texts in enumerate((texts_a, texts_b)):
        match = jnp.where(iota((sz.part, half), 1) + b * half == target, 2.0, 0.0)
        scores = strips[b] / own_rows + strips[b] / columns[b] - match
        grad = grad + dot(scores.astype(bf16), texts[...])
    own_row = iota((sz.part, sz.feat), 0) - (my_x >> 1)
    img_grad[...] = jnp.sum(jnp.where(own_row == 0, grad, 0.0), axis=0, keepdims=True)

    lane = iota((sz.nx, 64), 1)
    sub = iota((sz.nx, 64), 0)
    high, low = (pair >> 5).astype(f32), (pair & 31).astype(f32)
    found = []
    for table in names:
        hit = (table[:, :64] == high) & (table[:, 64:] == low) & (lane < sz.lines)

        def summed(value):
            value = jnp.where(hit, value, 0.0)
            return jnp.sum(jnp.sum(value, axis=0, keepdims=True), axis=1, keepdims=True)

        found.append([summed(v) for v in (lane.astype(f32), sub.astype(f32), jnp.ones((sz.nx, 64), f32))])
    found_line = (found[0][0] + found[1][0]).astype(i32)
    found_x = (found[0][1] + found[1][1]).astype(i32)
    found_core = jnp.where(found[1][2] > 0.5, 1 - my_core, my_core)
    named = position(found_line, found_x, found_core)
    strips = [exp_scores(near, images[...]) for images in (images_a, images_b)]
    own_columns = sum(jnp.sum(strip, axis=1, keepdims=True) for strip in strips)
    grad = jnp.zeros((sz.part, sz.feat), f32)
    for a, images in enumerate((images_a, images_b)):
        across = [jnp.transpose(jnp.broadcast_to(total, (tile, 128)))[0:1, :] for total in rows[a]]
        match = jnp.where(iota((sz.part, half), 1) + a * half == named, 2.0, 0.0)
        scores = strips[a] / jnp.concatenate(across, 1) + strips[a] / own_columns - match
        grad = grad + dot(scores.astype(bf16), images[...])
    txt_grad[...] = jnp.sum(jnp.where(own_row == sz.per, grad, 0.0), axis=0, keepdims=True)


def call(kernel, out_shape, in_specs=None, cost=None, limit=24, **kw):
    if cost is not None:
        kw["cost_estimate"] = pl.CostEstimate(flops=cost[0], bytes_accessed=cost[1], transcendentals=cost[2])
    if in_specs is not None:
        kw["in_specs"] = in_specs
    return pl.pallas_call(
        kernel,
        out_shape=out_shape,
        compiler_params=pltpu.CompilerParams(vmem_limit_bytes=limit << 20),
        **kw,
    )


def bind(kernel, *head):
    def bound(*refs):
        return kernel(*head, *refs)

    return bound


def rank_of(sz, y, z, x, core):
    return ((y * sz.nz + z) * sz.nx + x) * sz.cores + core


def split_groups(sz, first):
    width = 2 if first else 1
    groups = []
    for core in range(sz.cores):
        along_y = (core == 0) == first
        for fixed in range(sz.nz if along_y else sz.ny):
            for x in range(0, sz.nx, width):
                group = []
                for moving in range(sz.ny if along_y else sz.nz):
                    y, z = (moving, fixed) if along_y else (fixed, moving)
                    group += [rank_of(sz, y, z, x + b, core) for b in range(width)]
                groups.append(group)
    return groups


def per_device(
    image_tokens,
    text_tokens,
    text_counts,
    pair_labels,
    image_expert,
    image_rank,
    image_keep,
    text_expert,
    text_rank,
    text_keep,
    image_gate,
    text_gate,
    w_in,
    w_out,
):
    _, img_tok, feat = image_tokens.shape
    txt_tok = text_tokens.shape[1]
    sz = Sizes(lax.axis_size("expert"), lax.axis_size("dp"), img_tok, txt_tok, feat)
    img, txt = image_tokens[0], text_tokens[0]
    routes = (image_expert, image_rank, image_keep, text_expert, text_rank, text_keep)
    gates = (image_gate, text_gate)
    vmem = pl.BlockSpec(memory_space=pltpu.VMEM)
    smem = pl.BlockSpec(memory_space=pltpu.SMEM)

    def whole(shape):
        return pl.BlockSpec(shape, lambda i: (0, 0))

    hbm = pl.BlockSpec(memory_space=pltpu.HBM)

    def in_hbm(value):
        return pltpu.with_memory_space_constraint(value, pltpu.HBM)

    ff = w_in.shape[2]
    counts, keys = (1, img_tok), (1, txt_tok)
    packed, means, w_in_held = call(
        bind(dispatch_kernel, sz),
        (
            jax.ShapeDtypeStruct((sz.rows, feat), bf16),
            jax.ShapeDtypeStruct((8, feat), f32),
            jax.ShapeDtypeStruct((feat, ff), bf16),
        ),
        in_specs=[smem] * 2 + [hbm] * 11,
        out_specs=[vmem] * 3,
        scratch_shapes=[pltpu.VMEM(counts, i32)] * 3
        + [pltpu.VMEM(keys, i32)] * 3
        + [pltpu.VMEM(counts, f32), pltpu.VMEM(keys, f32)]
        + [pltpu.VMEM((img_tok, feat), bf16), pltpu.VMEM((txt_tok, feat), bf16)]
        + [pltpu.SemaphoreType.DMA((11,))],
        limit=16,
        name="dispatch",
    )(text_counts, pair_labels, *[in_hbm(v) for v in (*routes, *gates, img, txt, w_in[0])])

    def exchange(rows, count, axes="expert", groups=None):
        width = rows.shape[1]
        rows = rows.reshape(count, rows.shape[0] // count, width)
        rows = lax.all_to_all(
            rows, axes, split_axis=0, concat_axis=0, tiled=True, axis_index_groups=groups
        )
        return rows.reshape(-1, width)

    received = exchange(packed, sz.owners)
    back_rows = sz.owners * sz.back
    rows, labels = call(
        bind(expert_kernel, sz),
        (
            jax.ShapeDtypeStruct((back_rows, feat), bf16),
            jax.ShapeDtypeStruct((sz.part, 128), bf16),
        ),
        in_specs=[vmem, vmem, hbm, vmem],
        scratch_shapes=[pltpu.VMEM((ff, feat), bf16), pltpu.SemaphoreType.DMA],
        limit=28,
        name="expert",
    )(received, w_in_held, w_out[0], means)
    returned = exchange(rows, sz.owners)

    own, copies = call(
        bind(normalize_kernel, sz),
        (
            jax.ShapeDtypeStruct((sz.part, feat), bf16),
            jax.ShapeDtypeStruct((2 * sz.ny * sz.part, feat + 128), bf16),
        ),
        name="normalize",
    )(returned, labels)
    both = ("dp", "expert")
    got = exchange(copies, 2 * sz.ny, both, split_groups(sz, True))
    size = 2 * sz.ny * sz.nx + sz.nx
    copies = call(
        bind(merge_kernel, sz),
        jax.ShapeDtypeStruct((sz.nz * size, feat), bf16),
        name="merge",
    )(got)
    mine = exchange(copies, sz.nz, both, split_groups(sz, False))
    pairs = [(r, r ^ 1) for r in range(sz.pairs)]
    theirs = lax.ppermute(mine, both, pairs)
    img_out, txt_out = call(
        bind(combine_kernel, sz),
        (
            jax.ShapeDtypeStruct((img_tok, feat), bf16),
            jax.ShapeDtypeStruct((txt_tok, feat), bf16),
        ),
        cost=(2 * back_rows * (img_tok + txt_tok) * feat, 4 * back_rows * feat, 0),
        name="combine",
    )(*routes, *gates, img, txt, returned)
    halves = [jax.ShapeDtypeStruct((sz.half, feat), bf16)] * 2
    first = call(
        bind(first_head_kernel, sz),
        (
            *halves,
            jax.ShapeDtypeStruct((sz.nx, 128), f32),
            jax.ShapeDtypeStruct((sz.half, 1), f32),
            jax.ShapeDtypeStruct((1, sz.half), f32),
            jax.ShapeDtypeStruct((sz.part, sz.half), f32),
        ),
        cost=(2 * sz.half * sz.half * feat, 4 * sz.half * feat, sz.half * sz.half),
        name="first_head",
    )(own, mine)
    img_grad, txt_grad = call(
        bind(head_kernel, sz),
        (
            jax.ShapeDtypeStruct((1, feat), f32),
            jax.ShapeDtypeStruct((1, feat), f32),
        ),
        in_specs=[smem] + [vmem] * 8,
        scratch_shapes=[pltpu.VMEM((sz.half, feat), bf16)] * 2,
        name="head",
    )(pair_labels, own, theirs, *first)
    return (img_out[None], txt_out[None], img_grad, txt_grad)


def solution(mesh):
    both = ("dp", "expert")
    return jax.shard_map(
        per_device,
        mesh=mesh,
        in_specs=(
            P(both, None, None),
            P(both, None, None),
            P(both),
            P(both),
            P(both, None),
            P(both, None),
            P(both, None),
            P(both, None),
            P(both, None),
            P(both, None),
            P(both, None),
            P(both, None),
            P("expert", None, None),
            P("expert", None, None),
        ),
        out_specs=(
            P(both, None, None),
            P(both, None, None),
            P(both, None),
            P(both, None),
        ),
        check_vma=False,
    )
```

```python
import jax
import jax.numpy as jnp
import numpy as np
from jax import lax
from jax.experimental import pallas as pl
from jax.experimental.pallas import tpu as pltpu
from jax.sharding import PartitionSpec as P

logit_scale = 10.0
f32, bf16, i32 = jnp.float32, jnp.bfloat16, jnp.int32
NT = (((1,), (1,)), ((), ()))
TN = (((0,), (0,)), ((), ()))
NN = (((1,), (0,)), ((), ()))


def dot(left, right, dims=NN):
    return lax.dot_general(left, right, dims, preferred_element_type=f32)


def divided(value, by, limit):
    magic = -(-65536 // by)
    assert all((v * magic) >> 16 == v // by for v in range(limit))
    return (value * magic) >> 16


def iota(shape, dim):
    return lax.broadcasted_iota(i32, shape, dim)


def one_hot(mask):
    return jnp.where(mask, 1.0, 0.0).astype(bf16)


def three_parts(value):
    high = value.astype(bf16)
    rest = value - high.astype(f32)
    middle = rest.astype(bf16)
    low = (rest - middle.astype(f32)).astype(bf16)
    return high, middle, low


class Sizes:
    def __init__(self, owners, lines, img_tok, txt_tok, feat):
        self.owners, self.lines = owners, lines
        self.cores = 2
        self.nx = owners // self.cores
        self.ny = 1 << ((lines.bit_length() - 1 + 1) // 2)
        self.nz = lines // self.ny
        self.img_tok, self.txt_tok, self.feat = img_tok, txt_tok, feat
        self.cap = 5 * img_tok // (4 * owners)
        self.slots = self.cap + 2
        self.stride = -(-(self.slots + 2) // 8) * 8
        self.rows = owners * self.stride
        self.per = self.nx // 2
        self.part = 2 * self.per
        self.back = self.stride + self.part
        self.half = self.nx * lines
        self.pairs = owners * lines


def slot_masks(sz, stride, img_expert, img_rank, img_keep, txt_expert, txt_rank, txt_keep):
    img_target = img_expert * stride + img_rank
    txt_target = txt_expert * stride + sz.cap + txt_rank
    img_target = jnp.where(img_keep == 1, img_target, -1)
    txt_target = jnp.where(txt_keep == 1, txt_target, -1)
    return (
        one_hot(iota((sz.owners * stride, sz.img_tok), 0) == img_target),
        one_hot(iota((sz.owners * stride, sz.txt_tok), 0) == txt_target),
    )


def dispatch_kernel(sz, count_ref, label_ref, *refs):
    sources, (packed, means, weights_ref) = refs[:11], refs[11:14]
    held, sems = refs[14:24], refs[24]
    pairs = list(zip(sources, held))
    rows = weights_ref.shape[0] // 4
    for at in range(0, weights_ref.shape[0], rows):
        pairs.append((sources[10].at[at : at + rows, :], weights_ref.at[at : at + rows, :]))
    copies = [
        pltpu.make_async_copy(source, target, sems.at[i])
        for i, (source, target) in enumerate(pairs)
    ]
    for copy in copies:
        copy.start()
    for copy in copies[:10]:
        copy.wait()
    ie, ir, ik, te, tr, tk, ig, tg, img, txt = held
    img_mask, txt_mask = slot_masks(sz, sz.stride, ie[...], ir[...], ik[...], te[...], tr[...], tk[...])
    count, label = count_ref[0], label_ref[0]
    count_f = jnp.full((1, 1), count, i32).astype(f32)
    img_weight = jnp.where(ik[...] == 1, ig[...], 0.0) * (1.0 / sz.img_tok)
    valid = iota((1, sz.txt_tok), 1) < count
    txt_weight = jnp.where((tk[...] == 1) & valid, tg[...], 0.0) / count_f
    img_place = one_hot(iota((128, sz.img_tok), 0) == ir[...])
    txt_place = one_hot(iota((128, sz.txt_tok), 0) == tr[...] + sz.cap)
    img_at = iota((sz.owners, sz.img_tok), 0) == ie[...]
    txt_at = iota((sz.owners, sz.txt_tok), 0) == te[...]
    img_side = [jnp.where(img_at, part.astype(f32), 0.0) for part in three_parts(img_weight)]
    txt_side = [jnp.where(txt_at, part.astype(f32), 0.0) for part in three_parts(txt_weight)]
    table = dot(jnp.concatenate(img_side, 0).astype(bf16), img_place, NT)
    table = table + dot(jnp.concatenate(txt_side, 0).astype(bf16), txt_place, NT)
    tables = [table[at * sz.owners : (at + 1) * sz.owners] for at in range(3)]
    pad = sz.feat - 3 * 128
    if pad:
        tables.append(jnp.zeros((sz.owners, pad), f32))
    weights = jnp.concatenate(tables, 1).astype(bf16)
    lane = iota((sz.owners, sz.feat), 1)
    label_row = jnp.where(
        lane < 128,
        (label >> 5).astype(f32),
        jnp.where(lane < 256, (label & 31).astype(f32), 0.0),
    ).astype(bf16)
    row = iota((sz.rows, sz.owners), 0)
    block = iota((sz.rows, sz.owners), 1) * sz.stride
    out = dot(img_mask, img[...]) + dot(txt_mask, txt[...])
    out = out + dot(one_hot(row == block + sz.slots), weights)
    out = out + dot(one_hot(row == block + sz.slots + 1), label_row)
    packed[...] = out.astype(bf16)
    img_mean = dot(jnp.ones((8, sz.img_tok), bf16), img[...]) * (1.0 / sz.img_tok)
    counted = one_hot(iota((8, sz.txt_tok), 1) < count)
    txt_mean = dot(counted, txt[...]) / count_f
    means[...] = jnp.where(iota((8, sz.feat), 0) == 0, img_mean, txt_mean)
    for copy in copies[10:]:
        copy.wait()


def source_of(sz, r):
    bits = sz.per.bit_length() - 1
    parity, core = (r >> (bits + 1)) & 1, r >> (bits + 2)
    return ((r & (sz.per - 1)) * 2 + parity) * sz.cores + core


def gelu(x):
    return 0.5 * x * (1.0 + lax.erf(x * np.float32(np.sqrt(0.5))))


def expert_kernel(sz, x_ref, w_in, w_out_source, means, back_ref, label_ref, w_out, sem):
    copy = pltpu.make_async_copy(w_out_source, w_out, sem)
    copy.start()
    x = x_ref[...]
    hidden = gelu(dot(x, w_in[...])).astype(bf16)
    copy.wait()
    total = dot(hidden, w_out[...])
    out = total.astype(bf16)
    me = lax.axis_index("expert")
    line = lax.axis_index("dp")
    my_x, my_core = me >> 1, me & 1
    count = 2 * sz.owners
    r = iota((count, sz.rows), 0)
    c = iota((count, sz.rows), 1)
    block = divided(c, sz.stride, sz.rows)
    place = c - block * sz.stride
    is_txt = r & sz.per
    source = source_of(sz, r)
    r8 = iota((sz.part, sz.rows), 0)
    c8 = iota((sz.part, sz.rows), 1)
    named = (r8 * 2 + (my_x & 1)) * sz.cores + my_core
    wanted = (c8 == named * sz.stride + sz.slots + 1) & (r8 < sz.per)
    weighing = jnp.where(c == source * sz.stride + sz.slots, 1.0, 0.0)
    labelling = jnp.where(wanted, 1.0, 0.0)
    held = dot(jnp.concatenate([weighing, labelling], 0).astype(bf16), x)
    labels = held[count:, :]
    lane = iota((128, sz.rows), 1)
    lane_place = lane - divided(lane, sz.stride, sz.rows) * sz.stride
    spread = one_hot(iota((128, sz.rows), 0) == lane_place)
    own = (block == source) & (
        jnp.where(is_txt > 0, 1, 0) == jnp.where(place >= sz.cap, 1, 0)
    ) & (place < sz.slots)
    pieces = [held[:count, at : at + 128] for at in (0, 128, 256)]
    weight = dot(jnp.concatenate(pieces, 0).astype(bf16), spread)
    weight = jnp.where(jnp.concatenate([own] * 3, 0), weight, 0.0)
    pool = dot(weight.astype(bf16), out)
    pool = pool[:count] + pool[count : 2 * count] + pool[2 * count :]
    row = iota((count, sz.feat), 0)
    my_row = (my_core * 2 + (my_x & 1)) * sz.part + (my_x >> 1)
    pool = pool + jnp.where(row == my_row, means[0:1, :], 0.0)
    pool = pool + jnp.where(row == my_row + sz.per, means[1:2, :], 0.0)
    lost = pool - pool.astype(bf16).astype(f32)
    img_lost = jnp.sum(jnp.where(row == my_row, lost, 0.0), axis=0, keepdims=True)
    txt_lost = jnp.sum(jnp.where(row == my_row + sz.per, lost, 0.0), axis=0, keepdims=True)
    spare = iota((sz.stride, sz.feat), 0)
    blocks = []
    for e in range(sz.owners):
        kept = total[e * sz.stride : (e + 1) * sz.stride, :]
        kept = jnp.where(spare == sz.slots, img_lost, kept)
        blocks.append(jnp.where(spare == sz.slots + 1, txt_lost, kept))
        group = (e % sz.cores) * 2 + (e // sz.cores) % 2
        blocks.append(pool[group * sz.part : (group + 1) * sz.part, :])
    back_ref[...] = jnp.concatenate(blocks, 0).astype(bf16)
    lane = iota((sz.part, 128), 1)
    low = jnp.where(lane == line + 64, labels[:, 128:256], 0.0)
    label_ref[...] = jnp.where(lane == line, labels[:, :128], low).astype(bf16)


def normalize_kernel(sz, back, label, out, copies):
    me = lax.axis_index("expert")
    group = (me & 1) * 2 + ((me >> 1) & 1)
    shape = (sz.part, sz.owners * sz.back)
    r, c = iota(shape, 0), iota(shape, 1)
    owner = divided(c, sz.back, shape[1])
    place = c - owner * sz.back
    spare = jnp.where(r >= sz.per, sz.slots + 1, sz.slots)
    left = (place == spare) & (owner == source_of(sz, r + group * sz.part))
    pooled = dot(one_hot((place == sz.stride + r) | left), back[...])
    norm = jnp.sqrt(jnp.sum(pooled * pooled, axis=1, keepdims=True) + 1e-06)
    out[...] = (pooled / norm).astype(bf16)
    block = jnp.concatenate([out[...], label[...]], 1)
    for at in range(0, copies.shape[0], block.shape[0]):
        copies[at : at + block.shape[0], :] = block


def combine_kernel(sz, ie, ir, ik, te, tr, tk, ig, tg, img, txt, returned, img_out, txt_out):
    img_mask, txt_mask = slot_masks(sz, sz.back, ie[...], ir[...], ik[...], te[...], tr[...], tk[...])
    back = returned[...]
    for mask, gate, tokens, out in ((img_mask, ig, img, img_out), (txt_mask, tg, txt, txt_out)):
        count = tokens.shape[0]
        picked = dot(mask, back, TN)
        column = jnp.transpose(jnp.broadcast_to(gate[...], (128, count)))[:, 0:1]
        out[...] = (tokens[...].astype(f32) + column * picked).astype(bf16)


def merge_kernel(sz, got, copies):
    size = sz.part
    members = got.shape[0] // size
    count = members * sz.per
    bits = sz.per.bit_length() - 1
    shape = (2 * count + sz.nx, got.shape[0])
    r, c = iota(shape, 0), iota(shape, 1)
    is_txt = jnp.where(r >= count, 1, 0)
    pair = r - is_txt * count
    place = (pair >> bits) * size + is_txt * sz.per + (pair & (sz.per - 1))
    x = r - 2 * count
    label = ((c & (size - 1)) == (x >> 1)) & (((c >> (bits + 1)) & 1) == (x & 1))
    chosen = ((r >= 2 * count) & label) | ((r < 2 * count) & (c == place))
    all_rows = dot(one_hot(chosen), got[...]).astype(bf16)
    slabs = [all_rows[: 2 * count, at : at + 128] for at in range(0, sz.feat, 128)]
    block = jnp.concatenate(slabs + [all_rows[2 * count :, sz.feat :]], 0)
    for at in range(0, copies.shape[0], block.shape[0]):
        copies[at : at + block.shape[0], :] = block


def unpack(sz, got, images, texts):
    each = sz.half // sz.nz
    size = got.shape[0] // sz.nz
    table = jnp.zeros((sz.nx, 128), f32)
    for b in range(sz.nz):
        at, to = b * size, b * each
        for lane in range(0, sz.feat, 128):
            images[to : to + each, lane : lane + 128] = got[at : at + each, :]
            texts[to : to + each, lane : lane + 128] = got[at + each : at + 2 * each, :]
            at += 2 * each
        table = table + got[at : at + sz.nx, :].astype(f32)
    return table


def exp_scores(left, right):
    return jnp.exp(logit_scale * dot(left, right, NT))


def first_head_kernel(sz, own, mine, images, texts, table, row_totals, column_totals, image_strip, text_strip):
    half = sz.half
    table[...] = unpack(sz, mine, images, texts)
    tile = min(256, half)
    totals = jnp.zeros((1, half), f32)
    for at in range(0, half, tile):
        scores = exp_scores(images[at : at + tile, :], texts[...])
        row_totals[at : at + tile, :] = jnp.sum(scores, axis=1, keepdims=True)
        totals = totals + jnp.sum(scores, axis=0, keepdims=True)
    column_totals[...] = totals
    image_strip[...] = exp_scores(own[...], texts[...])
    text_strip[...] = exp_scores(own[...], images[...])


def head_kernel(
    sz, label_ref, own, theirs, images_a, texts_a, table_a, rows_a, columns_a, strip_a, text_strip_a,
    img_grad, txt_grad, images_b, texts_b,
):
    half = sz.half
    me = lax.axis_index("expert")
    line = lax.axis_index("dp")
    my_x, my_core = me >> 1, me & 1
    z_bits = sz.nz.bit_length() - 1
    pair = line * sz.owners + me

    def position(line, x, core):
        y, z = line >> z_bits, line & (sz.nz - 1)
        block = jnp.where(core == 0, z * sz.ny + y, y * sz.nz + z)
        place = (block * 2 + (x & 1)) * sz.per + (x >> 1)
        return jnp.where(core == my_core, 0, half) + place

    names = [table_a[...], unpack(sz, theirs, images_b, texts_b)]
    near = own[...]
    tile = min(256, half)
    columns = [columns_a[...], jnp.zeros((1, half), f32)]
    rows = [[rows_a[at : at + tile, :] for at in range(0, half, tile)], []]
    for t, at in enumerate(range(0, half, tile)):
        scores = exp_scores(images_a[at : at + tile, :], texts_b[...])
        rows[0][t] = rows[0][t] + jnp.sum(scores, axis=1, keepdims=True)
        columns[1] = columns[1] + jnp.sum(scores, axis=0, keepdims=True)
    for at in range(0, half, tile):
        total = jnp.zeros((tile, 1), f32)
        for b, texts in enumerate((texts_a, texts_b)):
            scores = exp_scores(images_b[at : at + tile, :], texts[...])
            total = total + jnp.sum(scores, axis=1, keepdims=True)
            columns[b] = columns[b] + jnp.sum(scores, axis=0, keepdims=True)
        rows[1].append(total)

    label = label_ref[0]
    owner = label & (sz.owners - 1)
    target = position(label >> (sz.owners.bit_length() - 1), owner >> 1, owner & 1)
    strips = [strip_a[...], exp_scores(near, texts_b[...])]
    own_rows = sum(jnp.sum(strip, axis=1, keepdims=True) for strip in strips)
    grad = jnp.zeros((sz.part, sz.feat), f32)
    for b, texts in enumerate((texts_a, texts_b)):
        match = jnp.where(iota((sz.part, half), 1) + b * half == target, 2.0, 0.0)
        scores = strips[b] / own_rows + strips[b] / columns[b] - match
        grad = grad + dot(scores.astype(bf16), texts[...])
    own_row = iota((sz.part, sz.feat), 0) - (my_x >> 1)
    img_grad[...] = jnp.sum(jnp.where(own_row == 0, grad, 0.0), axis=0, keepdims=True)

    lane = iota((sz.nx, 64), 1)
    sub = iota((sz.nx, 64), 0)
    high, low = (pair >> 5).astype(f32), (pair & 31).astype(f32)
    found = []
    for table in names:
        hit = (table[:, :64] == high) & (table[:, 64:] == low) & (lane < sz.lines)

        def summed(value):
            value = jnp.where(hit, value, 0.0)
            return jnp.sum(jnp.sum(value, axis=0, keepdims=True), axis=1, keepdims=True)

        found.append([summed(v) for v in (lane.astype(f32), sub.astype(f32), jnp.ones((sz.nx, 64), f32))])
    found_line = (found[0][0] + found[1][0]).astype(i32)
    found_x = (found[0][1] + found[1][1]).astype(i32)
    found_core = jnp.where(found[1][2] > 0.5, 1 - my_core, my_core)
    named = position(found_line, found_x, found_core)
    strips = [text_strip_a[...], exp_scores(near, images_b[...])]
    own_columns = sum(jnp.sum(strip, axis=1, keepdims=True) for strip in strips)
    grad = jnp.zeros((sz.part, sz.feat), f32)
    for a, images in enumerate((images_a, images_b)):
        across = [jnp.transpose(jnp.broadcast_to(total, (tile, 128)))[0:1, :] for total in rows[a]]
        match = jnp.where(iota((sz.part, half), 1) + a * half == named, 2.0, 0.0)
        scores = strips[a] / jnp.concatenate(across, 1) + strips[a] / own_columns - match
        grad = grad + dot(scores.astype(bf16), images[...])
    txt_grad[...] = jnp.sum(jnp.where(own_row == sz.per, grad, 0.0), axis=0, keepdims=True)


def call(kernel, out_shape, in_specs=None, cost=None, limit=24, **kw):
    if cost is not None:
        kw["cost_estimate"] = pl.CostEstimate(flops=cost[0], bytes_accessed=cost[1], transcendentals=cost[2])
    if in_specs is not None:
        kw["in_specs"] = in_specs
    return pl.pallas_call(
        kernel,
        out_shape=out_shape,
        compiler_params=pltpu.CompilerParams(vmem_limit_bytes=limit << 20),
        **kw,
    )


def bind(kernel, *head):
    def bound(*refs):
        return kernel(*head, *refs)

    return bound


def rank_of(sz, y, z, x, core):
    return ((y * sz.nz + z) * sz.nx + x) * sz.cores + core


def split_groups(sz, first):
    width = 2 if first else 1
    groups = []
    for core in range(sz.cores):
        along_y = (core == 0) == first
        for fixed in range(sz.nz if along_y else sz.ny):
            for x in range(0, sz.nx, width):
                group = []
                for moving in range(sz.ny if along_y else sz.nz):
                    y, z = (moving, fixed) if along_y else (fixed, moving)
                    group += [rank_of(sz, y, z, x + b, core) for b in range(width)]
                groups.append(group)
    return groups


def per_device(
    image_tokens,
    text_tokens,
    text_counts,
    pair_labels,
    image_expert,
    image_rank,
    image_keep,
    text_expert,
    text_rank,
    text_keep,
    image_gate,
    text_gate,
    w_in,
    w_out,
):
    _, img_tok, feat = image_tokens.shape
    txt_tok = text_tokens.shape[1]
    sz = Sizes(lax.axis_size("expert"), lax.axis_size("dp"), img_tok, txt_tok, feat)
    img, txt = image_tokens[0], text_tokens[0]
    routes = (image_expert, image_rank, image_keep, text_expert, text_rank, text_keep)
    gates = (image_gate, text_gate)
    vmem = pl.BlockSpec(memory_space=pltpu.VMEM)
    smem = pl.BlockSpec(memory_space=pltpu.SMEM)

    def whole(shape):
        return pl.BlockSpec(shape, lambda i: (0, 0))

    hbm = pl.BlockSpec(memory_space=pltpu.HBM)

    def in_hbm(value):
        return pltpu.with_memory_space_constraint(value, pltpu.HBM)

    ff = w_in.shape[2]
    counts, keys = (1, img_tok), (1, txt_tok)
    packed, means, w_in_held = call(
        bind(dispatch_kernel, sz),
        (
            jax.ShapeDtypeStruct((sz.rows, feat), bf16),
            jax.ShapeDtypeStruct((8, feat), f32),
            jax.ShapeDtypeStruct((feat, ff), bf16),
        ),
        in_specs=[smem] * 2 + [hbm] * 11,
        out_specs=[vmem] * 3,
        scratch_shapes=[pltpu.VMEM(counts, i32)] * 3
        + [pltpu.VMEM(keys, i32)] * 3
        + [pltpu.VMEM(counts, f32), pltpu.VMEM(keys, f32)]
        + [pltpu.VMEM((img_tok, feat), bf16), pltpu.VMEM((txt_tok, feat), bf16)]
        + [pltpu.SemaphoreType.DMA((14,))],
        limit=16,
        name="dispatch",
    )(text_counts, pair_labels, *[in_hbm(v) for v in (*routes, *gates, img, txt, w_in[0])])

    def exchange(rows, count, axes="expert", groups=None):
        width = rows.shape[1]
        rows = rows.reshape(count, rows.shape[0] // count, width)
        rows = lax.all_to_all(
            rows, axes, split_axis=0, concat_axis=0, tiled=True, axis_index_groups=groups
        )
        return rows.reshape(-1, width)

    received = exchange(packed, sz.owners)
    back_rows = sz.owners * sz.back
    rows, labels = call(
        bind(expert_kernel, sz),
        (
            jax.ShapeDtypeStruct((back_rows, feat), bf16),
            jax.ShapeDtypeStruct((sz.part, 128), bf16),
        ),
        in_specs=[vmem, vmem, hbm, vmem],
        scratch_shapes=[pltpu.VMEM((ff, feat), bf16), pltpu.SemaphoreType.DMA],
        limit=28,
        name="expert",
    )(received, w_in_held, w_out[0], means)
    returned = exchange(rows, sz.owners)

    own, copies = call(
        bind(normalize_kernel, sz),
        (
            jax.ShapeDtypeStruct((sz.part, feat), bf16),
            jax.ShapeDtypeStruct((2 * sz.ny * sz.part, feat + 128), bf16),
        ),
        name="normalize",
    )(returned, labels)
    both = ("dp", "expert")
    got = exchange(copies, 2 * sz.ny, both, split_groups(sz, True))
    size = 2 * sz.ny * sz.nx * (feat // 128) + sz.nx
    copies = call(
        bind(merge_kernel, sz),
        jax.ShapeDtypeStruct((sz.nz * size, 128), bf16),
        name="merge",
    )(got)
    mine = exchange(copies, sz.nz, both, split_groups(sz, False))
    pairs = [(r, r ^ 1) for r in range(sz.pairs)]
    theirs = lax.ppermute(mine, both, pairs)
    img_out, txt_out = call(
        bind(combine_kernel, sz),
        (
            jax.ShapeDtypeStruct((img_tok, feat), bf16),
            jax.ShapeDtypeStruct((txt_tok, feat), bf16),
        ),
        cost=(2 * back_rows * (img_tok + txt_tok) * feat, 4 * back_rows * feat, 0),
        name="combine",
    )(*routes, *gates, img, txt, returned)
    halves = [jax.ShapeDtypeStruct((sz.half, feat), bf16)] * 2
    first = call(
        bind(first_head_kernel, sz),
        (
            *halves,
            jax.ShapeDtypeStruct((sz.nx, 128), f32),
            jax.ShapeDtypeStruct((sz.half, 1), f32),
            jax.ShapeDtypeStruct((1, sz.half), f32),
            jax.ShapeDtypeStruct((sz.part, sz.half), f32),
            jax.ShapeDtypeStruct((sz.part, sz.half), f32),
        ),
        cost=(2 * sz.half * sz.half * feat, 4 * sz.half * feat, sz.half * sz.half),
        name="first_head",
    )(own, mine)
    img_grad, txt_grad = call(
        bind(head_kernel, sz),
        (
            jax.ShapeDtypeStruct((1, feat), f32),
            jax.ShapeDtypeStruct((1, feat), f32),
        ),
        in_specs=[smem] + [vmem] * 9,
        scratch_shapes=[pltpu.VMEM((sz.half, feat), bf16)] * 2,
        name="head",
    )(pair_labels, own, theirs, *first)
    return (img_out[None], txt_out[None], img_grad, txt_grad)


def solution(mesh):
    both = ("dp", "expert")
    return jax.shard_map(
        per_device,
        mesh=mesh,
        in_specs=(
            P(both, None, None),
            P(both, None, None),
            P(both),
            P(both),
            P(both, None),
            P(both, None),
            P(both, None),
            P(both, None),
            P(both, None),
            P(both, None),
            P(both, None),
            P(both, None),
            P("expert", None, None),
            P("expert", None, None),
        ),
        out_specs=(
            P(both, None, None),
            P(both, None, None),
            P(both, None),
            P(both, None),
        ),
        check_vma=False,
    )
```

```python
import jax
import jax.numpy as jnp
import numpy as np
from jax import lax
from jax.experimental import pallas as pl
from jax.experimental.pallas import tpu as pltpu
from jax.sharding import PartitionSpec as P

logit_scale = 10.0
f32, bf16, i32 = jnp.float32, jnp.bfloat16, jnp.int32
NT = (((1,), (1,)), ((), ()))
TN = (((0,), (0,)), ((), ()))
NN = (((1,), (0,)), ((), ()))


def dot(left, right, dims=NN):
    return lax.dot_general(left, right, dims, preferred_element_type=f32)


def divided(value, by, limit):
    magic = -(-65536 // by)
    assert all((v * magic) >> 16 == v // by for v in range(limit))
    return (value * magic) >> 16


def iota(shape, dim):
    return lax.broadcasted_iota(i32, shape, dim)


def one_hot(mask):
    return jnp.where(mask, 1.0, 0.0).astype(bf16)


def three_parts(value):
    high = value.astype(bf16)
    rest = value - high.astype(f32)
    middle = rest.astype(bf16)
    low = (rest - middle.astype(f32)).astype(bf16)
    return high, middle, low


class Sizes:
    def __init__(self, owners, lines, img_tok, txt_tok, feat):
        self.owners, self.lines = owners, lines
        self.cores = 2
        self.nx = owners // self.cores
        self.ny = 1 << ((lines.bit_length() - 1 + 1) // 2)
        self.nz = lines // self.ny
        self.img_tok, self.txt_tok, self.feat = img_tok, txt_tok, feat
        self.cap = 5 * img_tok // (4 * owners)
        self.slots = self.cap + 2
        self.stride = -(-(self.slots + 2) // 8) * 8
        self.rows = owners * self.stride
        self.per = self.nx // 2
        self.part = 2 * self.per
        self.back = self.stride + self.part
        self.half = self.nx * lines
        self.pairs = owners * lines


def slot_masks(sz, stride, img_expert, img_rank, img_keep, txt_expert, txt_rank, txt_keep):
    img_target = img_expert * stride + img_rank
    txt_target = txt_expert * stride + sz.cap + txt_rank
    img_target = jnp.where(img_keep == 1, img_target, -1)
    txt_target = jnp.where(txt_keep == 1, txt_target, -1)
    return (
        one_hot(iota((sz.owners * stride, sz.img_tok), 0) == img_target),
        one_hot(iota((sz.owners * stride, sz.txt_tok), 0) == txt_target),
    )


def dispatch_kernel(sz, count_ref, label_ref, *refs):
    sources, (packed, means, weights_ref) = refs[:11], refs[11:14]
    held, sems = refs[14:24], refs[24]
    pairs = list(zip(sources, held))
    rows = weights_ref.shape[0] // 4
    for at in range(0, weights_ref.shape[0], rows):
        pairs.append((sources[10].at[at : at + rows, :], weights_ref.at[at : at + rows, :]))
    copies = [
        pltpu.make_async_copy(source, target, sems.at[i])
        for i, (source, target) in enumerate(pairs)
    ]
    for copy in copies:
        copy.start()
    for copy in copies[:10]:
        copy.wait()
    ie, ir, ik, te, tr, tk, ig, tg, img, txt = held
    img_mask, txt_mask = slot_masks(sz, sz.stride, ie[...], ir[...], ik[...], te[...], tr[...], tk[...])
    count, label = count_ref[0], label_ref[0]
    count_f = jnp.full((1, 1), count, i32).astype(f32)
    img_weight = jnp.where(ik[...] == 1, ig[...], 0.0) * (1.0 / sz.img_tok)
    valid = iota((1, sz.txt_tok), 1) < count
    txt_weight = jnp.where((tk[...] == 1) & valid, tg[...], 0.0) / count_f
    img_place = one_hot(iota((128, sz.img_tok), 0) == ir[...])
    txt_place = one_hot(iota((128, sz.txt_tok), 0) == tr[...] + sz.cap)
    img_at = iota((sz.owners, sz.img_tok), 0) == ie[...]
    txt_at = iota((sz.owners, sz.txt_tok), 0) == te[...]
    img_side = [jnp.where(img_at, part.astype(f32), 0.0) for part in three_parts(img_weight)]
    txt_side = [jnp.where(txt_at, part.astype(f32), 0.0) for part in three_parts(txt_weight)]
    table = dot(jnp.concatenate(img_side, 0).astype(bf16), img_place, NT)
    table = table + dot(jnp.concatenate(txt_side, 0).astype(bf16), txt_place, NT)
    tables = [table[at * sz.owners : (at + 1) * sz.owners] for at in range(3)]
    pad = sz.feat - 3 * 128
    if pad:
        tables.append(jnp.zeros((sz.owners, pad), f32))
    weights = jnp.concatenate(tables, 1).astype(bf16)
    lane = iota((sz.owners, sz.feat), 1)
    label_row = jnp.where(
        lane < 128,
        (label >> 5).astype(f32),
        jnp.where(lane < 256, (label & 31).astype(f32), 0.0),
    ).astype(bf16)
    row = iota((sz.rows, sz.owners), 0)
    block = iota((sz.rows, sz.owners), 1) * sz.stride
    out = dot(img_mask, img[...]) + dot(txt_mask, txt[...])
    out = out + dot(one_hot(row == block + sz.slots), weights)
    out = out + dot(one_hot(row == block + sz.slots + 1), label_row)
    packed[...] = out.astype(bf16)
    img_mean = dot(jnp.ones((8, sz.img_tok), bf16), img[...]) * (1.0 / sz.img_tok)
    counted = one_hot(iota((8, sz.txt_tok), 1) < count)
    txt_mean = dot(counted, txt[...]) / count_f
    means[...] = jnp.where(iota((8, sz.feat), 0) == 0, img_mean, txt_mean)
    for copy in copies[10:]:
        copy.wait()


def source_of(sz, r):
    bits = sz.per.bit_length() - 1
    parity, core = (r >> (bits + 1)) & 1, r >> (bits + 2)
    return ((r & (sz.per - 1)) * 2 + parity) * sz.cores + core


def gelu(x):
    return 0.5 * x * (1.0 + lax.erf(x * np.float32(np.sqrt(0.5))))


def expert_kernel(sz, x_ref, w_in, w_out, means, back_ref, label_ref):
    x = x_ref[...]
    hidden = gelu(dot(x, w_in[...])).astype(bf16)
    total = dot(hidden, w_out[...])
    out = total.astype(bf16)
    me = lax.axis_index("expert")
    line = lax.axis_index("dp")
    my_x, my_core = me >> 1, me & 1
    count = 2 * sz.owners
    r = iota((count, sz.rows), 0)
    c = iota((count, sz.rows), 1)
    block = divided(c, sz.stride, sz.rows)
    place = c - block * sz.stride
    is_txt = r & sz.per
    source = source_of(sz, r)
    r8 = iota((sz.part, sz.rows), 0)
    c8 = iota((sz.part, sz.rows), 1)
    named = (r8 * 2 + (my_x & 1)) * sz.cores + my_core
    wanted = (c8 == named * sz.stride + sz.slots + 1) & (r8 < sz.per)
    weighing = jnp.where(c == source * sz.stride + sz.slots, 1.0, 0.0)
    labelling = jnp.where(wanted, 1.0, 0.0)
    held = dot(jnp.concatenate([weighing, labelling], 0).astype(bf16), x)
    labels = held[count:, :]
    lane = iota((128, sz.rows), 1)
    lane_place = lane - divided(lane, sz.stride, sz.rows) * sz.stride
    spread = one_hot(iota((128, sz.rows), 0) == lane_place)
    own = (block == source) & (
        jnp.where(is_txt > 0, 1, 0) == jnp.where(place >= sz.cap, 1, 0)
    ) & (place < sz.slots)
    pieces = [held[:count, at : at + 128] for at in (0, 128, 256)]
    weight = dot(jnp.concatenate(pieces, 0).astype(bf16), spread)
    weight = jnp.where(jnp.concatenate([own] * 3, 0), weight, 0.0)
    pool = dot(weight.astype(bf16), out)
    pool = pool[:count] + pool[count : 2 * count] + pool[2 * count :]
    row = iota((count, sz.feat), 0)
    my_row = (my_core * 2 + (my_x & 1)) * sz.part + (my_x >> 1)
    pool = pool + jnp.where(row == my_row, means[0:1, :], 0.0)
    pool = pool + jnp.where(row == my_row + sz.per, means[1:2, :], 0.0)
    lost = pool - pool.astype(bf16).astype(f32)
    img_lost = jnp.sum(jnp.where(row == my_row, lost, 0.0), axis=0, keepdims=True)
    txt_lost = jnp.sum(jnp.where(row == my_row + sz.per, lost, 0.0), axis=0, keepdims=True)
    spare = iota((sz.stride, sz.feat), 0)
    blocks = []
    for e in range(sz.owners):
        kept = total[e * sz.stride : (e + 1) * sz.stride, :]
        kept = jnp.where(spare == sz.slots, img_lost, kept)
        blocks.append(jnp.where(spare == sz.slots + 1, txt_lost, kept))
        group = (e % sz.cores) * 2 + (e // sz.cores) % 2
        blocks.append(pool[group * sz.part : (group + 1) * sz.part, :])
    back_ref[...] = jnp.concatenate(blocks, 0).astype(bf16)
    lane = iota((sz.part, 128), 1)
    low = jnp.where(lane == line + 64, labels[:, 128:256], 0.0)
    label_ref[...] = jnp.where(lane == line, labels[:, :128], low).astype(bf16)


def normalize_kernel(sz, back, label, out, copies):
    me = lax.axis_index("expert")
    group = (me & 1) * 2 + ((me >> 1) & 1)
    shape = (sz.part, sz.owners * sz.back)
    r, c = iota(shape, 0), iota(shape, 1)
    owner = divided(c, sz.back, shape[1])
    place = c - owner * sz.back
    spare = jnp.where(r >= sz.per, sz.slots + 1, sz.slots)
    left = (place == spare) & (owner == source_of(sz, r + group * sz.part))
    pooled = dot(one_hot((place == sz.stride + r) | left), back[...])
    norm = jnp.sqrt(jnp.sum(pooled * pooled, axis=1, keepdims=True) + 1e-06)
    out[...] = (pooled / norm).astype(bf16)
    block = jnp.concatenate([out[...], label[...]], 1)
    for at in range(0, copies.shape[0], block.shape[0]):
        copies[at : at + block.shape[0], :] = block


def combine_kernel(sz, ie, ir, ik, te, tr, tk, ig, tg, img, txt, returned, img_out, txt_out):
    img_mask, txt_mask = slot_masks(sz, sz.back, ie[...], ir[...], ik[...], te[...], tr[...], tk[...])
    back = returned[...]
    for mask, gate, tokens, out in ((img_mask, ig, img, img_out), (txt_mask, tg, txt, txt_out)):
        count = tokens.shape[0]
        picked = dot(mask, back, TN)
        column = jnp.transpose(jnp.broadcast_to(gate[...], (128, count)))[:, 0:1]
        out[...] = (tokens[...].astype(f32) + column * picked).astype(bf16)


def merge_kernel(sz, got, copies):
    size = sz.part
    members = got.shape[0] // size
    count = members * sz.per
    bits = sz.per.bit_length() - 1
    shape = (2 * count + sz.nx, got.shape[0])
    r, c = iota(shape, 0), iota(shape, 1)
    is_txt = jnp.where(r >= count, 1, 0)
    pair = r - is_txt * count
    place = (pair >> bits) * size + is_txt * sz.per + (pair & (sz.per - 1))
    x = r - 2 * count
    label = ((c & (size - 1)) == (x >> 1)) & (((c >> (bits + 1)) & 1) == (x & 1))
    chosen = ((r >= 2 * count) & label) | ((r < 2 * count) & (c == place))
    all_rows = dot(one_hot(chosen), got[...]).astype(bf16)
    slabs = [all_rows[: 2 * count, at : at + 128] for at in range(0, sz.feat, 128)]
    block = jnp.concatenate(slabs + [all_rows[2 * count :, sz.feat :]], 0)
    for at in range(0, copies.shape[0], block.shape[0]):
        copies[at : at + block.shape[0], :] = block


def unpack(sz, got, images, texts):
    each = sz.half // sz.nz
    size = got.shape[0] // sz.nz
    table = jnp.zeros((sz.nx, 128), f32)
    for b in range(sz.nz):
        at, to = b * size, b * each
        for lane in range(0, sz.feat, 128):
            images[to : to + each, lane : lane + 128] = got[at : at + each, :]
            texts[to : to + each, lane : lane + 128] = got[at + each : at + 2 * each, :]
            at += 2 * each
        table = table + got[at : at + sz.nx, :].astype(f32)
    return table


def exp_scores(left, right):
    return jnp.exp(logit_scale * dot(left, right, NT))


def along_lanes(column):
    tall = jnp.broadcast_to(column, (column.shape[0], 128))
    return jnp.transpose(tall)[0:1, :]


def first_head_kernel(sz, own, mine, images, texts, table, row_totals, column_totals, image_strip, text_strip):
    half = sz.half
    table[...] = unpack(sz, mine, images, texts)
    tile = min(256, half)
    totals = jnp.zeros((1, half), f32)
    for at in range(0, half, tile):
        scores = exp_scores(images[at : at + tile, :], texts[...])
        row_totals[at : at + tile, :] = jnp.sum(scores, axis=1, keepdims=True)
        totals = totals + jnp.sum(scores, axis=0, keepdims=True)
    column_totals[...] = totals
    image_strip[...] = exp_scores(own[...], texts[...])
    text_strip[...] = exp_scores(own[...], images[...])


def head_kernel(
    sz, label_ref, own, theirs, images_a, texts_a, table_a, rows_a, columns_a, strip_a, text_strip_a,
    img_grad, txt_grad, images_b, texts_b,
):
    half = sz.half
    me = lax.axis_index("expert")
    line = lax.axis_index("dp")
    my_x, my_core = me >> 1, me & 1
    z_bits = sz.nz.bit_length() - 1
    pair = line * sz.owners + me

    def position(line, x, core):
        y, z = line >> z_bits, line & (sz.nz - 1)
        block = jnp.where(core == 0, z * sz.ny + y, y * sz.nz + z)
        place = (block * 2 + (x & 1)) * sz.per + (x >> 1)
        return jnp.where(core == my_core, 0, half) + place

    names = [table_a[...], unpack(sz, theirs, images_b, texts_b)]
    near = own[...]
    tile = min(256, half)

    def against(left_halves, right):
        across, down = [], []
        for left in left_halves:
            total = jnp.zeros((1, half), f32)
            for at in range(0, half, tile):
                rows = left[at : at + tile, :]
                last = left is left_halves[-1] and at + tile == half
                scores = exp_scores(jnp.concatenate([rows, near], 0) if last else rows, right[...])
                own_scores = scores[tile:, :]
                scores = scores[:tile, :]
                across.append(along_lanes(jnp.sum(scores, axis=1, keepdims=True)))
                total = total + jnp.sum(scores, axis=0, keepdims=True)
            down.append(total)
        return jnp.concatenate(across, 1), down, own_scores

    rows_ab, (columns_ab,), strip_b = against([images_a], texts_b)
    columns_b, (rows_ba, rows_bb), text_strip_b = against([texts_a, texts_b], images_b)
    columns = [columns_a[...] + columns_b[:, :half], columns_ab + columns_b[:, half:]]
    rows = [along_lanes(rows_a[...]) + rows_ab, rows_ba + rows_bb]

    label = label_ref[0]
    owner = label & (sz.owners - 1)
    target = position(label >> (sz.owners.bit_length() - 1), owner >> 1, owner & 1)
    strips = [strip_a[...], strip_b]
    own_rows = sum(jnp.sum(strip, axis=1, keepdims=True) for strip in strips)
    grad = jnp.zeros((sz.part, sz.feat), f32)
    for b, texts in enumerate((texts_a, texts_b)):
        match = jnp.where(iota((sz.part, half), 1) + b * half == target, 2.0, 0.0)
        scores = strips[b] / own_rows + strips[b] / columns[b] - match
        grad = grad + dot(scores.astype(bf16), texts[...])
    own_row = iota((sz.part, sz.feat), 0) - (my_x >> 1)
    img_grad[...] = jnp.sum(jnp.where(own_row == 0, grad, 0.0), axis=0, keepdims=True)

    lane = iota((sz.nx, 64), 1)
    sub = iota((sz.nx, 64), 0)
    high, low = (pair >> 5).astype(f32), (pair & 31).astype(f32)
    found = []
    for table in names:
        hit = (table[:, :64] == high) & (table[:, 64:] == low) & (lane < sz.lines)

        def summed(value):
            value = jnp.where(hit, value, 0.0)
            return jnp.sum(jnp.sum(value, axis=0, keepdims=True), axis=1, keepdims=True)

        found.append([summed(v) for v in (lane.astype(f32), sub.astype(f32), jnp.ones((sz.nx, 64), f32))])
    found_line = (found[0][0] + found[1][0]).astype(i32)
    found_x = (found[0][1] + found[1][1]).astype(i32)
    found_core = jnp.where(found[1][2] > 0.5, 1 - my_core, my_core)
    named = position(found_line, found_x, found_core)
    strips = [text_strip_a[...], text_strip_b]
    own_columns = sum(jnp.sum(strip, axis=1, keepdims=True) for strip in strips)
    grad = jnp.zeros((sz.part, sz.feat), f32)
    for a, images in enumerate((images_a, images_b)):
        match = jnp.where(iota((sz.part, half), 1) + a * half == named, 2.0, 0.0)
        scores = strips[a] / rows[a] + strips[a] / own_columns - match
        grad = grad + dot(scores.astype(bf16), images[...])
    txt_grad[...] = jnp.sum(jnp.where(own_row == sz.per, grad, 0.0), axis=0, keepdims=True)


def call(kernel, out_shape, in_specs=None, cost=None, limit=24, **kw):
    if cost is not None:
        kw["cost_estimate"] = pl.CostEstimate(flops=cost[0], bytes_accessed=cost[1], transcendentals=cost[2])
    if in_specs is not None:
        kw["in_specs"] = in_specs
    return pl.pallas_call(
        kernel,
        out_shape=out_shape,
        compiler_params=pltpu.CompilerParams(vmem_limit_bytes=limit << 20),
        **kw,
    )


def bind(kernel, *head):
    def bound(*refs):
        return kernel(*head, *refs)

    return bound


def rank_of(sz, y, z, x, core):
    return ((y * sz.nz + z) * sz.nx + x) * sz.cores + core


def split_groups(sz, first):
    width = 2 if first else 1
    groups = []
    for core in range(sz.cores):
        along_y = (core == 0) == first
        for fixed in range(sz.nz if along_y else sz.ny):
            for x in range(0, sz.nx, width):
                group = []
                for moving in range(sz.ny if along_y else sz.nz):
                    y, z = (moving, fixed) if along_y else (fixed, moving)
                    group += [rank_of(sz, y, z, x + b, core) for b in range(width)]
                groups.append(group)
    return groups


def per_device(
    image_tokens,
    text_tokens,
    text_counts,
    pair_labels,
    image_expert,
    image_rank,
    image_keep,
    text_expert,
    text_rank,
    text_keep,
    image_gate,
    text_gate,
    w_in,
    w_out,
):
    _, img_tok, feat = image_tokens.shape
    txt_tok = text_tokens.shape[1]
    sz = Sizes(lax.axis_size("expert"), lax.axis_size("dp"), img_tok, txt_tok, feat)
    img, txt = image_tokens[0], text_tokens[0]
    routes = (image_expert, image_rank, image_keep, text_expert, text_rank, text_keep)
    gates = (image_gate, text_gate)
    vmem = pl.BlockSpec(memory_space=pltpu.VMEM)
    smem = pl.BlockSpec(memory_space=pltpu.SMEM)

    def whole(shape):
        return pl.BlockSpec(shape, lambda i: (0, 0))

    hbm = pl.BlockSpec(memory_space=pltpu.HBM)

    def in_hbm(value):
        return pltpu.with_memory_space_constraint(value, pltpu.HBM)

    ff = w_in.shape[2]
    counts, keys = (1, img_tok), (1, txt_tok)
    packed, means, w_in_held = call(
        bind(dispatch_kernel, sz),
        (
            jax.ShapeDtypeStruct((sz.rows, feat), bf16),
            jax.ShapeDtypeStruct((8, feat), f32),
            jax.ShapeDtypeStruct((feat, ff), bf16),
        ),
        in_specs=[smem] * 2 + [hbm] * 11,
        out_specs=[vmem] * 3,
        scratch_shapes=[pltpu.VMEM(counts, i32)] * 3
        + [pltpu.VMEM(keys, i32)] * 3
        + [pltpu.VMEM(counts, f32), pltpu.VMEM(keys, f32)]
        + [pltpu.VMEM((img_tok, feat), bf16), pltpu.VMEM((txt_tok, feat), bf16)]
        + [pltpu.SemaphoreType.DMA((14,))],
        limit=16,
        name="dispatch",
    )(text_counts, pair_labels, *[in_hbm(v) for v in (*routes, *gates, img, txt, w_in[0])])

    def exchange(rows, count, axes="expert", groups=None):
        width = rows.shape[1]
        rows = rows.reshape(count, rows.shape[0] // count, width)
        rows = lax.all_to_all(
            rows, axes, split_axis=0, concat_axis=0, tiled=True, axis_index_groups=groups
        )
        return rows.reshape(-1, width)

    received = exchange(packed, sz.owners)
    back_rows = sz.owners * sz.back
    rows, labels = call(
        bind(expert_kernel, sz),
        (
            jax.ShapeDtypeStruct((back_rows, feat), bf16),
            jax.ShapeDtypeStruct((sz.part, 128), bf16),
        ),
        in_specs=[vmem] * 4,
        limit=28,
        name="expert",
    )(received, w_in_held, w_out[0], means)
    returned = exchange(rows, sz.owners)

    own, copies = call(
        bind(normalize_kernel, sz),
        (
            jax.ShapeDtypeStruct((sz.part, feat), bf16),
            jax.ShapeDtypeStruct((2 * sz.ny * sz.part, feat + 128), bf16),
        ),
        name="normalize",
    )(returned, labels)
    both = ("dp", "expert")
    got = exchange(copies, 2 * sz.ny, both, split_groups(sz, True))
    size = 2 * sz.ny * sz.nx * (feat // 128) + sz.nx
    copies = call(
        bind(merge_kernel, sz),
        jax.ShapeDtypeStruct((sz.nz * size, 128), bf16),
        name="merge",
    )(got)
    mine = exchange(copies, sz.nz, both, split_groups(sz, False))
    pairs = [(r, r ^ 1) for r in range(sz.pairs)]
    theirs = lax.ppermute(mine, both, pairs)
    img_out, txt_out = call(
        bind(combine_kernel, sz),
        (
            jax.ShapeDtypeStruct((img_tok, feat), bf16),
            jax.ShapeDtypeStruct((txt_tok, feat), bf16),
        ),
        cost=(2 * back_rows * (img_tok + txt_tok) * feat, 4 * back_rows * feat, 0),
        name="combine",
    )(*routes, *gates, img, txt, returned)
    halves = [jax.ShapeDtypeStruct((sz.half, feat), bf16)] * 2
    first = call(
        bind(first_head_kernel, sz),
        (
            *halves,
            jax.ShapeDtypeStruct((sz.nx, 128), f32),
            jax.ShapeDtypeStruct((sz.half, 1), f32),
            jax.ShapeDtypeStruct((1, sz.half), f32),
            jax.ShapeDtypeStruct((sz.part, sz.half), f32),
            jax.ShapeDtypeStruct((sz.part, sz.half), f32),
        ),
        cost=(2 * sz.half * sz.half * feat, 4 * sz.half * feat, sz.half * sz.half),
        name="first_head",
    )(own, mine)
    img_grad, txt_grad = call(
        bind(head_kernel, sz),
        (
            jax.ShapeDtypeStruct((1, feat), f32),
            jax.ShapeDtypeStruct((1, feat), f32),
        ),
        in_specs=[smem] + [vmem] * 9,
        scratch_shapes=[pltpu.VMEM((sz.half, feat), bf16)] * 2,
        name="head",
    )(pair_labels, own, theirs, *first)
    return (img_out[None], txt_out[None], img_grad, txt_grad)


def solution(mesh):
    both = ("dp", "expert")
    return jax.shard_map(
        per_device,
        mesh=mesh,
        in_specs=(
            P(both, None, None),
            P(both, None, None),
            P(both),
            P(both),
            P(both, None),
            P(both, None),
            P(both, None),
            P(both, None),
            P(both, None),
            P(both, None),
            P(both, None),
            P(both, None),
            P("expert", None, None),
            P("expert", None, None),
        ),
        out_specs=(
            P(both, None, None),
            P(both, None, None),
            P(both, None),
            P(both, None),
        ),
        check_vma=False,
    )
```
